32 devices in a mesh: member: 4 (over z), domain: 8 (over y, x, core).
Axes of the slice: x: 2, y: 2, z: 4, core: 2. Of those that a mesh axis runs over, the one named last changes fastest.
Arguments:
- perturbations: bfloat16 [100, 16, 2048], P('member', None, 'domain'), may hold values from -0.59765625 to 0.59765625
- innovations: float32 [16, 2048], P(None, 'domain'), may hold values from -6 to 6
- precision_field: float32 [16, 2048], P(None, 'domain'), may hold values from 0.2 to 4
- obs_counts: int32 [2048], P('domain'), may hold values from 1 to 8
- vertical_map: float32 [16, 16], replicated, may hold values from -1.5 to 1.5
- diffusivity: float32 [16], replicated, may hold values from 0.05 to 0.24
Outputs:
- control: float32 [100, 16, 2048], P('member', None, 'domain')
- increment: float32 [16, 2048], P(None, 'domain')
The draws below stay inside these ranges and needn't reach their ends.
All inputs are finite; a program needn't handle non-finite values.
Results may differ from the reference program's by a relative error of at most 0.0003.
Values sent between devices are 32-bit elements; how exact they have to be, the bound alone decides.
No kernel may reach another device: no remote copies, remote signals or barrier semaphores. Data moves between devices by JAX's collectives and lax.ppermute only.
A program may use at most 64 MiB of HBM per device.

```python
import math
import jax
import jax.numpy as jnp
from jax import lax

L = 16
DIFF = 2
ITERS = 2
M = 100
H = 2048


def with_ends(result, own_key, smallest, high):
    longest = result.shape.index(max(result.shape))
    spots = []
    for shift in (0, 1):
        where = [jax.random.randint(jax.random.fold_in(own_key, axis), (), 0, length) for axis, length in enumerate(result.shape)]
        where[longest] = (where[longest] + shift) % result.shape[longest]
        spots.append(tuple(where))
    return result.at[spots[0]].set(smallest).at[spots[1]].set(high)


def shard_levels(rng, dims, split, low, top_value):
    gain = 1.0
    for axis_at, blocks in split:
        draws = jax.random.uniform(jax.random.fold_in(jax.random.fold_in(rng, 6), axis_at), (blocks,), jnp.float32, low / len(split), top_value / len(split))
        gain = gain * jnp.repeat(jnp.exp(draws), dims[axis_at] // blocks).reshape((-1,) + (1,) * (len(dims) - 1 - axis_at))
    return gain


def normal_values(stream_key, extent, scale, bound, split=(), kind=jnp.bfloat16):
    level = shard_levels(stream_key, extent, split, -0.22, 0.18) if split else 1.0
    drawn = jax.random.normal(stream_key, extent, jnp.float32) * scale * level
    return jnp.minimum(jnp.maximum(drawn, -bound), bound).astype(kind)


def setup_inputs(seed: int = 0) -> dict:
    arg_keys = jax.random.split(jax.random.key(seed), 7)
    return {
        "perturbations": normal_values(arg_keys[0], (M, L, H), 0.1, 0.59765625, ((0, 4), (2, 8))),
        "innovations": normal_values(arg_keys[1], (L, H), 1.0, 6.0, ((1, 8),), jnp.float32),
        "precision_field": jnp.clip(jnp.exp(math.log(4.0) - 2.9957323 * jax.random.uniform(arg_keys[2], (L, H), jnp.float32) ** shard_levels(arg_keys[2], (L, H), ((1, 8),), -0.2, 0.2)), 0.2, 4.0),
        "obs_counts": with_ends(jax.random.randint(arg_keys[3], (H,), 1, 9), jax.random.fold_in(arg_keys[3], 1), 1, 8).astype(jnp.int32),
        "vertical_map": normal_values(arg_keys[4], (L, L), L ** -0.5, 1.5, (), jnp.float32),
        "diffusivity": jnp.clip(jax.random.uniform(arg_keys[5], (L,), jnp.float32, 0.05, 0.24), 0.05, 0.24),
    }


def diffuse(field, diffusivity):
    coef = diffusivity[None, :, None]
    for step in range(DIFF):
        field = field + coef * (jnp.roll(field, 1, -1) - 2.0 * field + jnp.roll(field, -1, -1))
    return field


def forward(field, vertical_map, diffusivity):
    mixed = jnp.einsum("lk,mkh->mlh", vertical_map, field, precision=lax.Precision.HIGHEST)
    return diffuse(mixed, diffusivity)


def adjoint(field, vertical_map, diffusivity):
    smooth = diffuse(field, diffusivity)
    return jnp.einsum("kl,mkh->mlh", vertical_map, smooth, precision=lax.Precision.HIGHEST)


def reference(perturbations, innovations, precision_field, obs_counts, vertical_map, diffusivity):
    members = perturbations.astype(jnp.float32)
    weight = obs_counts.astype(jnp.float32)[None, :] * precision_field

    def ensemble(field):
        return jnp.sum(members * forward(field, vertical_map, diffusivity), axis=0)

    def hessian(field):
        weighted = weight * ensemble(field)
        return field + adjoint(members * weighted[None], vertical_map, diffusivity)

    rhs = adjoint(members * (weight * innovations)[None], vertical_map, diffusivity)
    control = jnp.zeros_like(rhs)
    residual = rhs
    direction = rhs
    norm_now = jnp.sum(residual * residual)
    for step in range(ITERS):
        image = hessian(direction)
        alpha = norm_now / jnp.sum(direction * image)
        control = control + alpha * direction
        residual = residual - alpha * image
        norm_next = jnp.sum(residual * residual)
        direction = residual + (norm_next / norm_now) * direction
        norm_now = norm_next
    return control, ensemble(control)
```

```python
import functools

import jax
import jax.numpy as jnp
from jax import lax
from jax.experimental import pallas as pl
from jax.experimental.pallas import tpu as pltpu
from jax.sharding import PartitionSpec as P

DIFF = 2
LANES = 128
HALO = 4 * DIFF
F32 = jnp.float32
HIGHEST = lax.Precision.HIGHEST
VMEM_LIMIT = 32 * 1024 * 1024


def lane_roll(value, shift):
    return pltpu.roll(value, shift % value.shape[-1], value.ndim - 1)


def lane_index(shape):
    return lax.broadcasted_iota(jnp.int32, shape, len(shape) - 1)


def level_column(diffusivity_ref, levels):
    row = lax.broadcasted_iota(jnp.int32, (levels, LANES), 0)
    column = jnp.zeros((levels, LANES), F32)
    for level in range(levels):
        column = jnp.where(row == level, diffusivity_ref[level], column)
    return column


def widen(column, like):
    copies = like.shape[-1] // LANES
    return column if copies == 1 else jnp.concatenate([column] * copies, axis=-1)


def smooth(field, coef):
    keep = 1.0 - 2.0 * coef
    for _ in range(DIFF):
        field = keep * field + coef * (lane_roll(field, 1) + lane_roll(field, -1))
    return field


def fill_columns(mix_ref, matrix):
    levels = matrix.shape[0]
    for k in range(levels):
        mix_ref[k] = jnp.broadcast_to(matrix[:, k : k + 1], (levels, LANES))


def mixed(mix_ref, field):
    levels = field.shape[0]
    out = None
    for k in range(levels):
        term = widen(mix_ref[k], field) * field[k : k + 1, :]
        out = term if out is None else out + term
    return out


def level_covariance(vertical_map):
    dims = (((1,), (1,)), ((), ()))
    return lax.dot_general(vertical_map, vertical_map, dims, precision=HIGHEST, preferred_element_type=F32)


def ensemble_square(members_ref, field, coef, mix_ref):
    coef = widen(coef, field)

    def one(m, total):
        p = members_ref[m].astype(F32)
        return total + p * smooth(mixed(mix_ref, smooth(p * field, coef)), coef)

    return lax.fori_loop(0, members_ref.shape[0], one, jnp.zeros(field.shape, F32), unroll=5)


def edge_from_own(field):
    lane = lane_index((field.shape[0], LANES))
    last = lane_roll(field[:, -LANES:], HALO)
    first = lane_roll(field[:, :LANES], LANES - HALO)
    return jnp.where(lane < HALO, last, jnp.where(lane >= LANES - HALO, first, 0.0))


def patch(main, edge, width):
    size = main.shape[-1]
    copies = size // LANES
    first = lane_roll(edge, HALO)
    last = lane_roll(edge, LANES - HALO)
    lane = lane_index(main.shape)
    out = jnp.where(lane < width, widen(first, main), main)
    return jnp.where(lane >= size - width, widen(last, main), out)


def weight_of(precision_ref, counts_ref):
    return counts_ref[...].astype(F32) * precision_ref[...]


def pack_kernel(members_ref, innovations_ref, precision_ref, counts_ref, first_ref, last_ref):
    count, levels, size = members_ref.shape
    lane = lane_index((levels, LANES))
    weight = weight_of(precision_ref, counts_ref)
    fields = (weight * innovations_ref[...], weight)

    def put(row, first, last):
        for ref, value, keep, shift in (
            (first_ref, first, lane < HALO, 0),
            (last_ref, last, lane >= LANES - HALO, HALO),
        ):
            value = jnp.where(keep, value, 0.0)
            value = pltpu.roll(value, shift, 1, stride=HALO, stride_axis=0)
            ref[row, :] = jnp.sum(value, axis=0)

    for m in range(count):
        put(m, members_ref[m, :, :LANES].astype(F32), members_ref[m, :, size - LANES :].astype(F32))
    for i, field in enumerate(fields):
        put(count + i, field[:, :LANES], field[:, size - LANES :])


def main_kernel(diffusivity_ref, members_ref, innovations_ref, precision_ref, counts_ref, map_ref, out_ref, mix_ref):
    levels = members_ref.shape[1]
    fill_columns(mix_ref, level_covariance(map_ref[...]))
    coef = level_column(diffusivity_ref, levels)
    source = weight_of(precision_ref, counts_ref) * innovations_ref[...]
    out_ref[...] = ensemble_square(members_ref, source, coef, mix_ref)


def edge_kernel(
    diffusivity_ref, members_ref, innovations_ref, precision_ref, counts_ref, map_ref, before_ref, after_ref, main_ref,
    edge_members_ref, edge_fields_ref, out_ref, mix_ref,
):
    count, levels, size = members_ref.shape
    fill_columns(mix_ref, level_covariance(map_ref[...]))
    coef = level_column(diffusivity_ref, levels)
    lane = lane_index((levels, LANES))
    weight = weight_of(precision_ref, counts_ref)
    fields = (weight * innovations_ref[...], weight)

    mine = lane // HALO == lax.broadcasted_iota(jnp.int32, (levels, LANES), 0)

    def repeated(value):
        value = jnp.where(mine, value, 0.0)
        shift = LANES // 2
        while shift >= HALO:
            value = value + lane_roll(value, shift)
            shift //= 2
        return value

    def unpacked(row, own):
        before, after = (
            repeated(jnp.broadcast_to(ref[row : row + 1, :], (levels, LANES))) for ref in (before_ref, after_ref)
        )
        value = jnp.where((lane >= HALO) & (lane < 2 * HALO), after, own)
        return jnp.where((lane >= LANES - 2 * HALO) & (lane < LANES - HALO), before, value)

    for m in range(count):
        ends = jnp.concatenate([members_ref[m, :, :LANES], members_ref[m, :, size - LANES :]], axis=-1).astype(F32)
        edge_members_ref[m] = unpacked(m, edge_from_own(ends)).astype(edge_members_ref.dtype)
    for i, field in enumerate(fields):
        edge_fields_ref[i] = unpacked(count + i, edge_from_own(field))
    edge = ensemble_square(edge_members_ref, edge_fields_ref[0], coef, mix_ref)
    out_ref[:, :size] = patch(main_ref[...], edge, HALO // 2)
    out_ref[:, size:] = edge


def tree_sum(own, others):
    a, b, c = (ref[...] for ref in others)
    return (own + a) + (b + c)


def second_kernel(
    diffusivity_ref, members_ref, precision_ref, counts_ref, map_ref, edge_members_ref, edge_fields_ref,
    own_ref, a_ref, b_ref, c_ref, first_ref, weighted_ref, out_ref, mix_ref,
):
    levels, size = precision_ref.shape
    fill_columns(mix_ref, level_covariance(map_ref[...]))
    coef = level_column(diffusivity_ref, levels)
    lane = lane_index((levels, LANES))
    total = tree_sum(own_ref[...], (a_ref, b_ref, c_ref))
    first, edge = total[:, :size], total[:, size:]
    own_lane = (lane < HALO) | (lane >= LANES - HALO)
    edge = jnp.where(own_lane, edge_from_own(first), edge)
    near = (lane < HALO + HALO // 2) | (lane >= LANES - HALO - HALO // 2)
    weighted = weight_of(precision_ref, counts_ref) * first
    edge_weighted = jnp.where(near, edge_fields_ref[1] * edge, 0.0)
    first_ref[...] = first
    weighted_ref[:, :size] = weighted
    weighted_ref[:, size:] = edge_weighted
    main = ensemble_square(members_ref, weighted, coef, mix_ref)
    edge = ensemble_square(edge_members_ref, edge_weighted, coef, mix_ref)
    out_ref[...] = patch(main, edge, HALO // 2)


def moments_kernel(
    innovations_ref, precision_ref, counts_ref, first_ref, weighted_ref, own_ref, a_ref, b_ref, c_ref,
    second_ref, moments_ref,
):
    levels, size = precision_ref.shape
    weight = weight_of(precision_ref, counts_ref)
    source = weight * innovations_ref[...]
    first, weighted = first_ref[...], weighted_ref[:, :size]
    second = tree_sum(own_ref[...], (a_ref, b_ref, c_ref))
    second_ref[...] = second
    lane = lane_index((1, LANES))
    width = LANES // 4
    out = jnp.zeros((1, LANES), F32)
    for i, product in enumerate((source * first, weighted * first, weighted * second, weight * second * second)):
        row = sum(product[:, at : at + LANES] for at in range(0, size, LANES))
        row = jnp.sum(row, axis=0, keepdims=True)
        row = row + lane_roll(row, LANES // 2)
        row = row + lane_roll(row, LANES // 4)
        out = jnp.where((lane >= i * width) & (lane < (i + 1) * width), row, out)
    moments_ref[...] = jnp.broadcast_to(out[None], moments_ref.shape)


def adjoint_kernel(diffusivity_ref, members_ref, edge_members_ref, map_ref, field_ref, edge_field_ref, out_ref, mix_ref):
    count, levels, size = members_ref.shape
    fill_columns(mix_ref, map_ref[...].T)
    coef = level_column(diffusivity_ref, levels)
    field, edge_field = field_ref[...], edge_field_ref[...]
    wide = widen(coef, field)

    def one(m, carry):
        main = smooth(members_ref[m].astype(F32) * field, wide)
        edge = smooth(edge_members_ref[m].astype(F32) * edge_field, coef)
        out_ref[m] = mixed(mix_ref, patch(main, edge, DIFF))
        return carry

    lax.fori_loop(0, count, one, 0, unroll=5)


def final_kernel(moments_ref, start_ref, image_ref, first_ref, second_ref, control_ref, increment_ref):
    lane = lane_index((1, LANES))
    width = LANES // 4
    row = jnp.sum(moments_ref[...], axis=0)
    sums = [
        jnp.sum(jnp.where((lane >= i * width) & (lane < (i + 1) * width), row, 0.0), axis=1, keepdims=True)
        for i in range(4)
    ]
    m1, m2, m3 = (value / sums[0] for value in sums[1:])
    alpha = 1.0 / (1.0 + m1)
    spread = jnp.maximum(m2 - m1 * m1, 0.0)
    bend = jnp.maximum(m3 - 2.0 * m1 * m2 + m1 * m1 * m1, 0.0)
    beta = alpha * alpha * spread
    below = spread + bend - alpha * spread * spread
    usable = (spread > 0.0) & (below > 0.0)
    later = jnp.where(usable, jnp.minimum(spread / jnp.where(usable, below, 1.0), 1.0), 0.0)
    on_start = alpha + later * (alpha * m1 + beta)
    on_image = -later * alpha
    increment_ref[...] = on_start * first_ref[...] + on_image * second_ref[...]
    for m in range(start_ref.shape[0]):
        control_ref[m] = on_start * start_ref[m] + on_image * image_ref[m]


def vmem():
    return pl.BlockSpec(memory_space=pltpu.VMEM)


def smem():
    return pl.BlockSpec(memory_space=pltpu.SMEM)


def call(kernel, name, out_shape, args, levels=None, scalars=False, flops=0):
    specs = [vmem()] * len(args)
    if scalars:
        specs[0] = smem()
    scratch = [] if levels is None else [pltpu.VMEM((levels, levels, LANES), F32)]
    multiple = isinstance(out_shape, (list, tuple))
    moved = sum(a.size * a.dtype.itemsize for a in (*args, *(out_shape if multiple else (out_shape,))))
    return pl.pallas_call(
        kernel,
        name=name,
        out_shape=out_shape,
        in_specs=specs,
        out_specs=[vmem()] * len(out_shape) if multiple else vmem(),
        scratch_shapes=scratch,
        cost_estimate=pl.CostEstimate(flops=flops, bytes_accessed=moved, transcendentals=0),
        compiler_params=pltpu.CompilerParams(vmem_limit_bytes=VMEM_LIMIT),
    )(*args)


def shape_of(*dims, dtype=F32):
    return jax.ShapeDtypeStruct(dims, dtype)


def from_partners(value, axis):
    size = lax.axis_size(axis)
    return [lax.ppermute(value, axis, [(i, i ^ step) for i in range(size)]) for step in range(1, size)]


def local(perturbations, innovations, precision_field, obs_counts, vertical_map, diffusivity):
    count, levels, size = perturbations.shape
    counts = obs_counts.reshape(1, size)
    rows = -(-(count + 2) // 8) * 8
    domains = lax.axis_size("domain")
    fields = (innovations, precision_field, counts)
    up = [(i, (i + 1) % domains) for i in range(domains)]
    down = [(j, i) for i, j in up]

    first_cells, last_cells = call(
        pack_kernel, "pack_edges", [shape_of(rows, LANES)] * 2, (perturbations, *fields), flops=count * levels * LANES
    )
    before = lax.ppermute(last_cells, "domain", up)
    after = lax.ppermute(first_cells, "domain", down)
    work = count * levels * size * 60
    main = call(
        main_kernel, "first_inner", shape_of(levels, size), (diffusivity, perturbations, *fields, vertical_map),
        levels, True, work,
    )
    edge_members, edge_fields, part = call(
        edge_kernel, "first_edges",
        [shape_of(count, levels, LANES, dtype=perturbations.dtype), shape_of(2, levels, LANES), shape_of(levels, size + LANES)],
        (diffusivity, perturbations, *fields, vertical_map, before, after, main), levels, True, work,
    )
    others = from_partners(part, "member")
    source = precision_field * counts.astype(F32) * innovations

    def adjoint(name, field, edge_field):
        return call(
            adjoint_kernel, name, shape_of(count, levels, size),
            (diffusivity, perturbations, edge_members, vertical_map, field, edge_field), levels, True, work,
        )

    start = adjoint("start_vector", source, edge_fields[0])
    first, weighted, part = call(
        second_kernel, "second_apply", [shape_of(levels, size), shape_of(levels, size + LANES), shape_of(levels, size)],
        (diffusivity, perturbations, precision_field, counts, vertical_map, edge_members, edge_fields, part, *others),
        levels, True, work,
    )
    others = from_partners(part, "member")
    image = adjoint("image_vector", weighted[:, :size], weighted[:, size:])
    second, moments = call(
        moments_kernel, "moments", [shape_of(levels, size), shape_of(domains, 1, LANES)],
        (*fields, first, weighted, part, *others),
    )
    moments = lax.all_to_all(moments, "domain", 0, 0)
    return tuple(
        call(
            final_kernel, "combine", [shape_of(count, levels, size), shape_of(levels, size)],
            (moments, start, image, first, second),
        )
    )


def solution(mesh):
    in_specs = (
        P("member", None, "domain"),
        P(None, "domain"),
        P(None, "domain"),
        P("domain"),
        P(),
        P(),
    )
    out_specs = (P("member", None, "domain"), P(None, "domain"))
    return jax.shard_map(local, mesh=mesh, in_specs=in_specs, out_specs=out_specs, check_vma=False)
```

```python
import functools

import jax
import jax.numpy as jnp
from jax import lax
from jax.experimental import pallas as pl
from jax.experimental.pallas import tpu as pltpu
from jax.sharding import PartitionSpec as P

DIFF = 2
LANES = 128
REACH = 2 * DIFF
HALO = 2 * REACH
SLOT = 4 * HALO
SLOTS = LANES // SLOT
F32 = jnp.float32
HIGHEST = lax.Precision.HIGHEST
VMEM_LIMIT = 32 * 1024 * 1024


def lane_roll(value, shift):
    return pltpu.roll(value, shift % value.shape[-1], value.ndim - 1)


def lane_index(shape):
    return lax.broadcasted_iota(jnp.int32, shape, len(shape) - 1)


def widen(column, like):
    copies = like.shape[-1] // LANES
    return column if copies == 1 else jnp.concatenate([column] * copies, axis=-1)


def level_column(diffusivity_ref, levels):
    row = lax.broadcasted_iota(jnp.int32, (levels, LANES), 0)
    column = jnp.zeros((levels, LANES), F32)
    for level in range(levels):
        column = jnp.where(row == level, diffusivity_ref[level], column)
    return column


def smooth(field, taps):
    near = lane_roll(field, 1) + lane_roll(field, -1)
    far = lane_roll(field, 2) + lane_roll(field, -2)
    return taps[0] * field + taps[1] * near + taps[2] * far


def mixed(mix_ref, field_ref):
    out = None
    for k in range(mix_ref.shape[0]):
        row = field_ref[k : k + 1, :]
        term = widen(mix_ref[k], row) * row
        out = term if out is None else out + term
    return out


def wide_taps(taps_ref, like):
    return [widen(taps_ref[i], like) for i in range(3)]


def apply_ensemble(parts, taps_ref, mix_ref, scratches):
    totals = []
    for (members_ref, field), (x_ref, y_ref) in zip(parts, scratches):
        taps = wide_taps(taps_ref, field)
        for m in range(members_ref.shape[0]):
            x_ref[m] = smooth(members_ref[m].astype(F32) * field, taps)
    for (members_ref, field), (x_ref, y_ref) in zip(parts, scratches):
        for m in range(members_ref.shape[0]):
            y_ref[m] = mixed(mix_ref, x_ref.at[m])
    for (members_ref, field), (x_ref, y_ref) in zip(parts, scratches):
        taps = wide_taps(taps_ref, field)
        total = jnp.zeros(field.shape, F32)
        for m in range(members_ref.shape[0]):
            total = total + members_ref[m].astype(F32) * smooth(y_ref[m], taps)
        totals.append(total)
    return totals


def all_slots(value):
    shift = SLOT
    while shift < LANES:
        value = value + lane_roll(value, shift)
        shift *= 2
    return value


def ends_of(first, last, lane):
    return jnp.where(lane < HALO, first, jnp.where(lane >= LANES - HALO, last, 0.0))


def patch(main, edge, width, slot=0):
    size = main.shape[-1]
    first = lane_roll(edge, -(slot * SLOT + HALO))
    last = lane_roll(edge, -(slot * SLOT + 3 * HALO))
    lane = lane_index(main.shape)
    out = jnp.where(lane < width, widen(first, main), main)
    return jnp.where(lane >= size - width, widen(last, main), out)


def pack_kernel(
    members_hbm, innovations_hbm, precision_hbm, counts_hbm,
    members_ref, fields_ref, low_ref, high_ref, innovations_ref, precision_ref, counts_ref, sems,
):
    copies = [
        pltpu.make_async_copy(source, target, sems.at[i])
        for i, (source, target) in enumerate(
            (
                (members_hbm, members_ref),
                (innovations_hbm, innovations_ref),
                (precision_hbm, precision_ref),
                (counts_hbm, counts_ref),
            )
        )
    ]
    for copy in copies:
        copy.start()
    for copy in copies[1:]:
        copy.wait()
    weight = counts_ref[...].astype(F32) * precision_ref[...]
    fields_ref[0] = weight * innovations_ref[...]
    fields_ref[1] = weight
    copies[0].wait()
    count, levels, size = members_ref.shape
    lane = lane_index((levels, LANES))
    for tile in range(low_ref.shape[0]):
        low, high = jnp.zeros((levels, LANES), F32), jnp.zeros((levels, LANES), F32)
        for slot in range(SLOTS):
            m = tile * SLOTS + slot
            if m < count:
                first, last = members_ref[m, :, :LANES].astype(F32), members_ref[m, :, size - LANES :].astype(F32)
            elif m < count + 2:
                first, last = fields_ref[m - count, :, :LANES], fields_ref[m - count, :, size - LANES :]
            else:
                continue
            ends = ends_of(first, last, lane)
            low = low + lane_roll(ends, slot * SLOT + HALO)
            high = high + lane_roll(ends, slot * SLOT + 3 * HALO)
        low_ref[tile] = low
        high_ref[tile] = high


def main_kernel(
    diffusivity_ref, map_ref, members_ref, fields_ref, taps_ref, square_ref, adjoint_ref, out_ref, x_ref, y_ref
):
    levels = members_ref.shape[1]
    matrix = map_ref[...]
    dims = (((1,), (1,)), ((), ()))
    square = lax.dot_general(matrix, matrix, dims, precision=HIGHEST, preferred_element_type=F32)
    turned = matrix.T
    for k in range(levels):
        square_ref[k] = jnp.broadcast_to(square[:, k : k + 1], (levels, LANES))
        adjoint_ref[k] = jnp.broadcast_to(turned[:, k : k + 1], (levels, LANES))
    coef = level_column(diffusivity_ref, levels)
    keep = 1.0 - 2.0 * coef
    taps_ref[0] = keep * keep + 2.0 * coef * coef
    taps_ref[1] = 2.0 * keep * coef
    taps_ref[2] = coef * coef
    (out_ref[...],) = apply_ensemble([(members_ref, fields_ref[0])], taps_ref, square_ref, [(x_ref, y_ref)])


def edge_kernel(
    count, low_ref, high_ref, before_ref, after_ref, taps_ref, square_ref, main_ref,
    edge_members_ref, edge_fields_ref, out_ref, x_ref, y_ref,
):
    tiles, levels, _ = low_ref.shape
    size = main_ref.shape[1]
    lane = lane_index((levels, LANES))
    at, slot_of = lane % SLOT, lane // SLOT
    for tile in range(tiles):
        own = jnp.where(at >= 2 * HALO, high_ref[tile], low_ref[tile])
        value = jnp.where(at >= 3 * HALO, after_ref[tile], jnp.where(at < HALO, before_ref[tile], own))
        for i in range(2):
            place, slot = divmod(count + i, SLOTS)
            if place == tile:
                edge_fields_ref[i] = all_slots(jnp.where(slot_of == slot, value, 0.0))
        held = min(max(count - tile * SLOTS, 0), SLOTS)
        edge_members_ref[tile] = value if held == SLOTS else jnp.where(slot_of < held, value, 0.0)
    (edge,) = apply_ensemble([(edge_members_ref, edge_fields_ref[0])], taps_ref, square_ref, [(x_ref, y_ref)])
    edge = all_slots(edge)
    out_ref[:, :size] = patch(main_ref[...], edge, REACH)
    out_ref[:, size:] = edge


def tree_sum(own_ref, a_ref, b_ref, c_ref):
    return (own_ref[...] + a_ref[...]) + (b_ref[...] + c_ref[...])


def second_kernel(
    members_ref, edge_members_ref, fields_ref, edge_fields_ref, taps_ref, square_ref, own_ref, a_ref, b_ref, c_ref, _,
    first_ref, weighted_ref, edge_weighted_ref, out_ref, x_ref, y_ref, edge_x_ref, edge_y_ref,
):
    _, levels, size = members_ref.shape
    lane = lane_index((levels, LANES))
    at = lane % SLOT
    total = tree_sum(own_ref, a_ref, b_ref, c_ref)
    first, edge = total[:, :size], total[:, size:]
    ends = ends_of(first[:, :LANES], first[:, size - LANES :], lane)
    own = jnp.where(lane >= 2 * HALO, lane_roll(ends, 3 * HALO), lane_roll(ends, HALO))
    own = all_slots(jnp.where(lane < SLOT, own, 0.0))
    edge = jnp.where((at >= HALO) & (at < 3 * HALO), own, edge)
    weighted = fields_ref[1] * first
    edge_weighted = edge_fields_ref[1] * edge
    first_ref[...] = first
    weighted_ref[...] = weighted
    edge_weighted_ref[...] = edge_weighted
    main, edge = apply_ensemble(
        [(members_ref, weighted), (edge_members_ref, edge_weighted)], taps_ref, square_ref,
        [(x_ref, y_ref), (edge_x_ref, edge_y_ref)],
    )
    out_ref[...] = patch(main, all_slots(edge), REACH)


def moments_kernel(
    fields_ref, first_ref, weighted_ref, own_ref, a_ref, b_ref, c_ref, _, second_ref, moments_ref
):
    size = first_ref.shape[1]
    source, weight = fields_ref[0], fields_ref[1]
    first, weighted = first_ref[...], weighted_ref[...]
    second = tree_sum(own_ref, a_ref, b_ref, c_ref)
    second_ref[...] = second
    lane = lane_index((1, LANES))
    width = LANES // 4
    out = jnp.zeros((1, LANES), F32)
    for i, product in enumerate((source * first, weighted * first, weighted * second, weight * second * second)):
        row = sum(product[:, at : at + LANES] for at in range(0, size, LANES))
        row = jnp.sum(row, axis=0, keepdims=True)
        row = row + lane_roll(row, LANES // 2)
        row = row + lane_roll(row, LANES // 4)
        out = jnp.where((lane >= i * width) & (lane < (i + 1) * width), row, out)
    moments_ref[...] = jnp.broadcast_to(out[None], moments_ref.shape)


def adjoint_kernel(
    members_ref, edge_members_ref, field_ref, edge_field_ref, taps_ref, adjoint_ref, out_ref, x_ref, edge_x_ref
):
    field, edge_field = field_ref[...], edge_field_ref[...]
    taps, edge_taps = wide_taps(taps_ref, field), wide_taps(taps_ref, edge_field)
    for tile in range(edge_members_ref.shape[0]):
        edge_x_ref[tile] = smooth(edge_members_ref[tile] * edge_field, edge_taps)
    for m in range(members_ref.shape[0]):
        main = smooth(members_ref[m].astype(F32) * field, taps)
        x_ref[m] = patch(main, edge_x_ref[m // SLOTS], DIFF, m % SLOTS)
    for m in range(members_ref.shape[0]):
        out_ref[m] = mixed(adjoint_ref, x_ref.at[m])


def final_kernel(moments_ref, start_ref, image_ref, first_ref, second_ref, control_ref, increment_ref):
    lane = lane_index((1, LANES))
    width = LANES // 4
    row = jnp.sum(moments_ref[...], axis=0)
    sums = [
        jnp.sum(jnp.where((lane >= i * width) & (lane < (i + 1) * width), row, 0.0), axis=1, keepdims=True)
        for i in range(4)
    ]
    m1, m2, m3 = (value / sums[0] for value in sums[1:])
    alpha = 1.0 / (1.0 + m1)
    spread = jnp.maximum(m2 - m1 * m1, 0.0)
    bend = jnp.maximum(m3 - 2.0 * m1 * m2 + m1 * m1 * m1, 0.0)
    beta = alpha * alpha * spread
    below = spread + bend - alpha * spread * spread
    usable = (spread > 0.0) & (below > 0.0)
    later = jnp.where(usable, jnp.minimum(spread / jnp.where(usable, below, 1.0), 1.0), 0.0)
    on_start = alpha + later * (alpha * m1 + beta)
    on_image = -later * alpha
    increment_ref[...] = on_start * first_ref[...] + on_image * second_ref[...]
    for m in range(start_ref.shape[0]):
        control_ref[m] = on_start * start_ref[m] + on_image * image_ref[m]


def vmem():
    return pl.BlockSpec(memory_space=pltpu.VMEM)


def elsewhere():
    return pl.BlockSpec(memory_space=pl.ANY)


def smem():
    return pl.BlockSpec(memory_space=pltpu.SMEM)


def call(kernel, name, outs, args, scratch=(), specs=None, flops=0):
    specs = specs or {}
    moved = sum(a.size * a.dtype.itemsize for a in (*args, *outs))
    return pl.pallas_call(
        kernel,
        name=name,
        out_shape=list(outs),
        in_specs=[specs.get(i, vmem)() for i in range(len(args))],
        out_specs=[vmem()] * len(outs),
        scratch_shapes=list(scratch),
        cost_estimate=pl.CostEstimate(flops=flops, bytes_accessed=moved, transcendentals=0),
        compiler_params=pltpu.CompilerParams(vmem_limit_bytes=VMEM_LIMIT),
    )(*args)


def shape_of(*dims, dtype=F32):
    return jax.ShapeDtypeStruct(dims, dtype)


def from_partners(value, axis):
    size = lax.axis_size(axis)
    return [lax.ppermute(value, axis, [(i, i ^ step) for i in range(size)]) for step in range(1, size)]


def local(perturbations, innovations, precision_field, obs_counts, vertical_map, diffusivity):
    count, levels, size = perturbations.shape
    tiles = -(-(count + 2) // SLOTS)
    domains = lax.axis_size("domain")
    up = [(i, (i + 1) % domains) for i in range(domains)]
    down = [(j, i) for i, j in up]
    level = shape_of(levels, size)
    members_f32 = shape_of(count, levels, size)
    edge_tiles = shape_of(tiles, levels, LANES)
    column = shape_of(levels, levels, LANES)
    work, edge_work = count * levels * size * 50, tiles * levels * LANES * 50
    scratch = [pltpu.VMEM((count, levels, size), F32)] * 2
    edge_scratch = [pltpu.VMEM((tiles, levels, LANES), F32)] * 2

    members, fields, low, high = call(
        pack_kernel, "pack_edges",
        [shape_of(count, levels, size, dtype=perturbations.dtype), shape_of(2, levels, size), edge_tiles, edge_tiles],
        (perturbations, innovations, precision_field, obs_counts.reshape(1, size)),
        [pltpu.VMEM((levels, size), F32)] * 2 + [pltpu.VMEM((1, size), jnp.int32), pltpu.SemaphoreType.DMA((4,))],
        dict.fromkeys(range(4), elsewhere), tiles * levels * LANES * 20,
    )
    before = lax.ppermute(low, "domain", up)
    after = lax.ppermute(high, "domain", down)
    taps, square, mapped, main = call(
        main_kernel, "first_inner", [shape_of(3, levels, LANES), column, column, level],
        (diffusivity, vertical_map, members, fields), scratch, {0: smem}, work,
    )
    edge_members, edge_fields, part = call(
        functools.partial(edge_kernel, count), "first_edges",
        [edge_tiles, shape_of(2, levels, LANES), shape_of(levels, size + LANES)],
        (low, high, before, after, taps, square, main), edge_scratch, flops=edge_work,
    )

    def adjoint(name, field, edge_field):
        (out,) = call(
            adjoint_kernel, name, [members_f32], (members, edge_members, field, edge_field, taps, mapped),
            [scratch[0], edge_scratch[0]], flops=work,
        )
        return out

    others = from_partners(part, "member")
    start = adjoint("start_vector", fields[0], edge_fields[0])
    first, weighted, edge_weighted, part = call(
        second_kernel, "second_apply", [level, level, shape_of(levels, LANES), level],
        (members, edge_members, fields, edge_fields, taps, square, part, *others, start),
        scratch + edge_scratch, {10: elsewhere}, work + edge_work,
    )
    others = from_partners(part, "member")
    image = adjoint("image_vector", weighted, edge_weighted)
    second, moments = call(
        moments_kernel, "moments", [level, shape_of(domains, 1, LANES)],
        (fields, first, weighted, part, *others, image), (), {7: elsewhere},
    )
    moments = lax.all_to_all(moments, "domain", 0, 0)
    return tuple(
        call(final_kernel, "combine", [members_f32, level], (moments, start, image, first, second))
    )


def solution(mesh):
    in_specs = (
        P("member", None, "domain"),
        P(None, "domain"),
        P(None, "domain"),
        P("domain"),
        P(),
        P(),
    )
    out_specs = (P("member", None, "domain"), P(None, "domain"))
    return jax.shard_map(local, mesh=mesh, in_specs=in_specs, out_specs=out_specs, check_vma=False)
```

```python
import functools

import jax
import jax.numpy as jnp
from jax import lax
from jax.experimental import pallas as pl
from jax.experimental.pallas import tpu as pltpu
from jax.sharding import PartitionSpec as P

DIFF = 2
LANES = 128
REACH = 2 * DIFF
HALO = 2 * REACH
SLOT = 4 * HALO
SLOTS = LANES // SLOT
F32 = jnp.float32
HIGHEST = lax.Precision.HIGHEST
VMEM_LIMIT = 32 * 1024 * 1024


def lane_roll(value, shift):
    return pltpu.roll(value, shift % value.shape[-1], value.ndim - 1)


def lane_index(shape):
    return lax.broadcasted_iota(jnp.int32, shape, len(shape) - 1)


def widen(column, like):
    copies = like.shape[-1] // LANES
    return column if copies == 1 else jnp.concatenate([column] * copies, axis=-1)


def level_column(row):
    levels = row.shape[1]
    square = jnp.broadcast_to(row, (levels, levels))
    own = lax.broadcasted_iota(jnp.int32, square.shape, 0) == lane_index(square.shape)
    return jnp.broadcast_to(jnp.sum(jnp.where(own, square, 0.0), axis=1, keepdims=True), (levels, LANES))


def smooth(field, taps):
    near = lane_roll(field, 1) + lane_roll(field, -1)
    far = lane_roll(field, 2) + lane_roll(field, -2)
    return taps[0] * field + taps[1] * near + taps[2] * far


def mixed(mix_ref, field_ref):
    out = None
    for k in range(mix_ref.shape[0]):
        row = field_ref[k : k + 1, :]
        term = widen(mix_ref[k], row) * row
        out = term if out is None else out + term
    return out


def wide_taps(taps_ref, like):
    return [widen(taps_ref[i], like) for i in range(3)]


def apply_ensemble(parts, taps_ref, mix_ref, scratches):
    totals = []
    for (members_ref, field), (x_ref, y_ref) in zip(parts, scratches):
        taps = wide_taps(taps_ref, field)
        for m in range(members_ref.shape[0]):
            x_ref[m] = smooth(members_ref[m].astype(F32) * field, taps)
    for (members_ref, field), (x_ref, y_ref) in zip(parts, scratches):
        for m in range(members_ref.shape[0]):
            y_ref[m] = mixed(mix_ref, x_ref.at[m])
    for (members_ref, field), (x_ref, y_ref) in zip(parts, scratches):
        taps = wide_taps(taps_ref, field)
        total = jnp.zeros(field.shape, F32)
        for m in range(members_ref.shape[0]):
            total = total + members_ref[m].astype(F32) * smooth(y_ref[m], taps)
        totals.append(total)
    return totals


def all_slots(value):
    shift = SLOT
    while shift < LANES:
        value = value + lane_roll(value, shift)
        shift *= 2
    return value


def ends_of(first, last, lane):
    return jnp.where(lane < HALO, first, jnp.where(lane >= LANES - HALO, last, 0.0))


def added(total, term):
    return term if total is None else total + term


def patch(main, edge, width, slot=0):
    size = main.shape[-1]
    first = lane_roll(edge, -(slot * SLOT + HALO))
    last = lane_roll(edge, -(slot * SLOT + 3 * HALO))
    lane = lane_index(main.shape)
    out = jnp.where(lane < width, widen(first, main), main)
    return jnp.where(lane >= size - width, widen(last, main), out)


def pack_kernel(
    members_hbm, innovations_hbm, precision_hbm, counts_hbm,
    low_ref, high_ref, low_message_ref, high_message_ref,
    members_ref, innovations_ref, precision_ref, counts_ref, sems,
):
    copies = [
        pltpu.make_async_copy(source, target, sems.at[i])
        for i, (source, target) in enumerate(
            (
                (members_hbm, members_ref),
                (innovations_hbm, innovations_ref),
                (precision_hbm, precision_ref),
                (counts_hbm, counts_ref),
            )
        )
    ]
    for copy in copies:
        copy.start()
    for copy in copies[1:]:
        copy.wait()
    weight = counts_ref[...].astype(F32) * precision_ref[...]
    fields = (weight * innovations_ref[...], weight)
    copies[0].wait()
    count, levels, size = members_ref.shape
    lane = lane_index((levels, LANES))
    at = lane % SLOT
    low_message, high_message = [None] * low_message_ref.shape[0], [None] * low_message_ref.shape[0]
    for tile in range(low_ref.shape[0]):
        low = high = None
        for slot in range(SLOTS):
            m = tile * SLOTS + slot
            if m < count:
                first, last = members_ref[m, :, :LANES].astype(F32), members_ref[m, :, size - LANES :].astype(F32)
            elif m < count + 2:
                first, last = fields[m - count][:, :LANES], fields[m - count][:, size - LANES :]
            else:
                continue
            ends = ends_of(first, last, lane)
            low = added(low, lane_roll(ends, slot * SLOT + HALO))
            high = added(high, lane_roll(ends, slot * SLOT + 3 * HALO))
        low_ref[tile] = low
        high_ref[tile] = high
        place, shift = divmod(tile, SLOT // HALO)
        low_message[place] = added(low_message[place], lane_roll(jnp.where(at < HALO, low, 0.0), shift * HALO))
        high = lane_roll(jnp.where(at >= 3 * HALO, high, 0.0), shift * HALO - 3 * HALO)
        high_message[place] = added(high_message[place], high)
    for place in range(low_message_ref.shape[0]):
        low_message_ref[place] = low_message[place]
        high_message_ref[place] = high_message[place]


def main_kernel(
    diffusivity_ref, map_ref, members_ref, innovations_ref, precision_ref, counts_ref,
    taps_ref, square_ref, adjoint_ref, source_ref, weight_ref, out_ref, x_ref, y_ref,
):
    levels = members_ref.shape[1]
    matrix = map_ref[...]
    dims = (((1,), (1,)), ((), ()))
    square = lax.dot_general(matrix, matrix, dims, precision=HIGHEST, preferred_element_type=F32)
    turned = matrix.T
    for k in range(levels):
        square_ref[k] = jnp.broadcast_to(square[:, k : k + 1], (levels, LANES))
        adjoint_ref[k] = jnp.broadcast_to(turned[:, k : k + 1], (levels, LANES))
    coef = level_column(diffusivity_ref[...])
    keep = 1.0 - 2.0 * coef
    taps_ref[0] = keep * keep + 2.0 * coef * coef
    taps_ref[1] = 2.0 * keep * coef
    taps_ref[2] = coef * coef
    weight = counts_ref[...].astype(F32) * precision_ref[...]
    source = weight * innovations_ref[...]
    source_ref[...], weight_ref[...] = source, weight
    (out_ref[...],) = apply_ensemble([(members_ref, source)], taps_ref, square_ref, [(x_ref, y_ref)])


def edge_kernel(
    count, low_ref, high_ref, before_ref, after_ref, taps_ref, square_ref, main_ref,
    edge_members_ref, edge_source_ref, edge_weight_ref, out_ref, x_ref, y_ref,
):
    tiles, levels, _ = low_ref.shape
    size = main_ref.shape[1]
    lane = lane_index((levels, LANES))
    at, slot_of = lane % SLOT, lane // SLOT
    for tile in range(tiles):
        place, shift = divmod(tile, SLOT // HALO)
        before = lane_roll(before_ref[place], -shift * HALO)
        after = lane_roll(after_ref[place], (3 - shift) * HALO)
        own = jnp.where(at >= 2 * HALO, high_ref[tile], low_ref[tile])
        value = jnp.where(at >= 3 * HALO, after, jnp.where(at < HALO, before, own))
        for i, field_ref in enumerate((edge_source_ref, edge_weight_ref)):
            place, slot = divmod(count + i, SLOTS)
            if place == tile:
                field_ref[...] = all_slots(jnp.where(slot_of == slot, value, 0.0))
        held = min(max(count - tile * SLOTS, 0), SLOTS)
        edge_members_ref[tile] = value if held == SLOTS else jnp.where(slot_of < held, value, 0.0)
    (edge,) = apply_ensemble([(edge_members_ref, edge_source_ref[...])], taps_ref, square_ref, [(x_ref, y_ref)])
    edge = all_slots(edge)
    out_ref[:, :size] = patch(main_ref[...], edge, REACH)
    out_ref[:, size:] = edge


def tree_sum(own_ref, a_ref, b_ref, c_ref):
    return (own_ref[...] + a_ref[...]) + (b_ref[...] + c_ref[...])


def second_kernel(
    members_ref, edge_members_ref, weight_ref, edge_weight_ref, taps_ref, square_ref, own_ref, a_ref, b_ref, c_ref, _,
    first_ref, weighted_ref, edge_weighted_ref, out_ref, x_ref, y_ref, edge_x_ref, edge_y_ref,
):
    _, levels, size = members_ref.shape
    lane = lane_index((levels, LANES))
    at = lane % SLOT
    total = tree_sum(own_ref, a_ref, b_ref, c_ref)
    first, edge = total[:, :size], total[:, size:]
    ends = ends_of(first[:, :LANES], first[:, size - LANES :], lane)
    own = jnp.where(lane >= 2 * HALO, lane_roll(ends, 3 * HALO), lane_roll(ends, HALO))
    own = all_slots(jnp.where(lane < SLOT, own, 0.0))
    edge = jnp.where((at >= HALO) & (at < 3 * HALO), own, edge)
    weighted = weight_ref[...] * first
    edge_weighted = edge_weight_ref[...] * edge
    first_ref[...] = first
    weighted_ref[...] = weighted
    edge_weighted_ref[...] = edge_weighted
    main, edge = apply_ensemble(
        [(members_ref, weighted), (edge_members_ref, edge_weighted)], taps_ref, square_ref,
        [(x_ref, y_ref), (edge_x_ref, edge_y_ref)],
    )
    out_ref[...] = patch(main, all_slots(edge), REACH)


def moments_kernel(
    source_ref, weight_ref, first_ref, weighted_ref, own_ref, a_ref, b_ref, c_ref, _, second_ref, moments_ref
):
    size = first_ref.shape[1]
    source, weight = source_ref[...], weight_ref[...]
    first, weighted = first_ref[...], weighted_ref[...]
    second = tree_sum(own_ref, a_ref, b_ref, c_ref)
    second_ref[...] = second
    lane = lane_index((1, LANES))
    width = LANES // 4
    out = jnp.zeros((1, LANES), F32)
    for i, product in enumerate((source * first, weighted * first, weighted * second, weight * second * second)):
        row = sum(product[:, at : at + LANES] for at in range(0, size, LANES))
        row = jnp.sum(row, axis=0, keepdims=True)
        row = row + lane_roll(row, LANES // 2)
        row = row + lane_roll(row, LANES // 4)
        out = jnp.where((lane >= i * width) & (lane < (i + 1) * width), row, out)
    moments_ref[...] = out


def adjoint_kernel(
    members_ref, edge_members_ref, field_ref, edge_field_ref, taps_ref, adjoint_ref, out_ref, x_ref, edge_x_ref
):
    field, edge_field = field_ref[...], edge_field_ref[...]
    taps, edge_taps = wide_taps(taps_ref, field), wide_taps(taps_ref, edge_field)
    for tile in range(edge_members_ref.shape[0]):
        edge_x_ref[tile] = smooth(edge_members_ref[tile] * edge_field, edge_taps)
    for m in range(members_ref.shape[0]):
        main = smooth(members_ref[m].astype(F32) * field, taps)
        x_ref[m] = patch(main, edge_x_ref[m // SLOTS], DIFF, m % SLOTS)
    for m in range(members_ref.shape[0]):
        out_ref[m] = mixed(adjoint_ref, x_ref.at[m])


def final_kernel(
    own_ref, a_ref, b_ref, c_ref, start_ref, image_ref, first_ref, second_ref, control_ref, increment_ref
):
    lane = lane_index((1, LANES))
    width = LANES // 4
    row = tree_sum(own_ref, a_ref, b_ref, c_ref)
    sums = [
        jnp.sum(jnp.where((lane >= i * width) & (lane < (i + 1) * width), row, 0.0), axis=1, keepdims=True)
        for i in range(4)
    ]
    m1, m2, m3 = (value / sums[0] for value in sums[1:])
    alpha = 1.0 / (1.0 + m1)
    spread = jnp.maximum(m2 - m1 * m1, 0.0)
    bend = jnp.maximum(m3 - 2.0 * m1 * m2 + m1 * m1 * m1, 0.0)
    beta = alpha * alpha * spread
    below = spread + bend - alpha * spread * spread
    usable = (spread > 0.0) & (below > 0.0)
    later = jnp.where(usable, jnp.minimum(spread / jnp.where(usable, below, 1.0), 1.0), 0.0)
    on_start = alpha + later * (alpha * m1 + beta)
    on_image = -later * alpha
    increment_ref[...] = on_start * first_ref[...] + on_image * second_ref[...]
    for m in range(start_ref.shape[0]):
        control_ref[m] = on_start * start_ref[m] + on_image * image_ref[m]


def vmem():
    return pl.BlockSpec(memory_space=pltpu.VMEM)


def elsewhere():
    return pl.BlockSpec(memory_space=pl.ANY)


def call(kernel, name, outs, args, scratch=(), specs=None, flops=0, limit=VMEM_LIMIT):
    specs = specs or {}
    moved = sum(a.size * a.dtype.itemsize for a in (*args, *outs))
    return pl.pallas_call(
        kernel,
        name=name,
        out_shape=list(outs),
        in_specs=[specs.get(i, vmem)() for i in range(len(args))],
        out_specs=[vmem()] * len(outs),
        scratch_shapes=list(scratch),
        cost_estimate=pl.CostEstimate(flops=flops, bytes_accessed=moved, transcendentals=0),
        compiler_params=pltpu.CompilerParams(vmem_limit_bytes=limit),
    )(*args)


def shape_of(*dims, dtype=F32):
    return jax.ShapeDtypeStruct(dims, dtype)


def from_partners(value, axis):
    size = lax.axis_size(axis)
    return [lax.ppermute(value, axis, [(i, i ^ step) for i in range(size)]) for step in range(1, size)]


def partner(value, axis, step):
    return lax.ppermute(value, axis, [(i, i ^ step) for i in range(lax.axis_size(axis))])


def domain_terms(value, axis):
    size = lax.axis_size(axis)
    value, step = value + partner(value, axis, 1), 2
    while 4 * step < size:
        if (size // step).bit_length() % 2:
            terms = [partner(value, axis, k * step) for k in (1, 2, 3)]
            value, step = (value + terms[0]) + (terms[1] + terms[2]), 4 * step
        else:
            value, step = value + partner(value, axis, step), 2 * step
    return [value, *(partner(value, axis, k * step) for k in (1, 2, 3))]


def local(perturbations, innovations, precision_field, obs_counts, vertical_map, diffusivity):
    count, levels, size = perturbations.shape
    tiles = -(-(count + 2) // SLOTS)
    domains = lax.axis_size("domain")
    up = [(i, (i + 1) % domains) for i in range(domains)]
    down = [(j, i) for i, j in up]
    level = shape_of(levels, size)
    members_f32 = shape_of(count, levels, size)
    edge_tiles = shape_of(tiles, levels, LANES)
    edge_row = shape_of(1, LANES)
    edge_level = shape_of(levels, LANES)
    message = shape_of(-(-tiles * HALO // SLOT), levels, LANES)
    column = shape_of(levels, levels, LANES)
    work, edge_work = count * levels * size * 50, tiles * levels * LANES * 50
    scratch = [pltpu.VMEM((count, levels, size), F32)] * 2
    edge_scratch = [pltpu.VMEM((tiles, levels, LANES), F32)] * 2

    counts = obs_counts.reshape(1, size)
    low, high, low_message, high_message = call(
        pack_kernel, "pack_edges", [edge_tiles, edge_tiles, message, message],
        (perturbations, innovations, precision_field, counts),
        [
            pltpu.VMEM((count, levels, size), perturbations.dtype), pltpu.VMEM((levels, size), F32),
            pltpu.VMEM((levels, size), F32), pltpu.VMEM((1, size), jnp.int32), pltpu.SemaphoreType.DMA((4,)),
        ],
        dict.fromkeys(range(4), elsewhere), tiles * levels * LANES * 20, None,
    )
    before = lax.ppermute(low_message, "domain", up)
    after = lax.ppermute(high_message, "domain", down)
    taps, square, mapped, source, weight, main = call(
        main_kernel, "first_inner", [shape_of(3, levels, LANES), column, column, level, level, level],
        (diffusivity.reshape(1, levels), vertical_map, perturbations, innovations, precision_field, counts),
        scratch, flops=work,
    )
    edge_members, edge_source, edge_weight, part = call(
        functools.partial(edge_kernel, count), "first_edges",
        [edge_tiles, edge_level, edge_level, shape_of(levels, size + LANES)],
        (low, high, before, after, taps, square, main), edge_scratch, flops=edge_work,
    )

    def adjoint(name, field, edge_field):
        (out,) = call(
            adjoint_kernel, name, [members_f32], (perturbations, edge_members, field, edge_field, taps, mapped),
            [scratch[0], edge_scratch[0]], flops=work,
        )
        return out

    others = from_partners(part, "member")
    start = adjoint("start_vector", source, edge_source)
    first, weighted, edge_weighted, part = call(
        second_kernel, "second_apply", [level, level, edge_level, level],
        (perturbations, edge_members, weight, edge_weight, taps, square, part, *others, start),
        scratch + edge_scratch, {10: elsewhere}, work + edge_work,
    )
    others = from_partners(part, "member")
    image = adjoint("image_vector", weighted, edge_weighted)
    second, moments = call(
        moments_kernel, "moments", [level, edge_row],
        (source, weight, first, weighted, part, *others, image), (), {8: elsewhere},
    )
    moments = domain_terms(moments, "domain")
    return tuple(
        call(final_kernel, "combine", [members_f32, level], (*moments, start, image, first, second))
    )


def solution(mesh):
    in_specs = (
        P("member", None, "domain"),
        P(None, "domain"),
        P(None, "domain"),
        P("domain"),
        P(),
        P(),
    )
    out_specs = (P("member", None, "domain"), P(None, "domain"))
    return jax.shard_map(local, mesh=mesh, in_specs=in_specs, out_specs=out_specs, check_vma=False)
```

```python
import functools

import jax
import jax.numpy as jnp
from jax import lax
from jax.experimental import pallas as pl
from jax.experimental.pallas import tpu as pltpu
from jax.sharding import PartitionSpec as P

DIFF = 2
LANES = 128
REACH = 2 * DIFF
HALO = 2 * REACH
SLOT = 4 * HALO
SLOTS = LANES // SLOT
F32 = jnp.float32
HIGHEST = lax.Precision.HIGHEST
VMEM_LIMIT = 32 * 1024 * 1024


def lane_roll(value, shift):
    return pltpu.roll(value, shift % value.shape[-1], value.ndim - 1)


def lane_index(shape):
    return lax.broadcasted_iota(jnp.int32, shape, len(shape) - 1)


def widen(column, like):
    copies = like.shape[-1] // LANES
    return column if copies == 1 else jnp.concatenate([column] * copies, axis=-1)


def level_column(row):
    levels = row.shape[1]
    square = jnp.broadcast_to(row, (levels, levels))
    own = lax.broadcasted_iota(jnp.int32, square.shape, 0) == lane_index(square.shape)
    return jnp.broadcast_to(jnp.sum(jnp.where(own, square, 0.0), axis=1, keepdims=True), (levels, LANES))


def smooth(field, taps):
    near = lane_roll(field, 1) + lane_roll(field, -1)
    far = lane_roll(field, 2) + lane_roll(field, -2)
    return taps[0] * field + taps[1] * near + taps[2] * far


def mixed(mix_ref, field_ref):
    out = None
    for k in range(mix_ref.shape[0]):
        row = field_ref[k : k + 1, :]
        term = widen(mix_ref[k], row) * row
        out = term if out is None else out + term
    return out


def wide_taps(taps_ref, like):
    return [widen(taps_ref[i], like) for i in range(3)]


def apply_ensemble(parts, taps_ref, mix_ref, scratches):
    totals = []
    for (members_ref, field), (x_ref, y_ref) in zip(parts, scratches):
        taps = wide_taps(taps_ref, field)
        for m in range(members_ref.shape[0]):
            x_ref[m] = smooth(members_ref[m].astype(F32) * field, taps)
    for (members_ref, field), (x_ref, y_ref) in zip(parts, scratches):
        for m in range(members_ref.shape[0]):
            y_ref[m] = mixed(mix_ref, x_ref.at[m])
    for (members_ref, field), (x_ref, y_ref) in zip(parts, scratches):
        taps = wide_taps(taps_ref, field)
        total = jnp.zeros(field.shape, F32)
        for m in range(members_ref.shape[0]):
            total = total + members_ref[m].astype(F32) * smooth(y_ref[m], taps)
        totals.append(total)
    return totals


def all_slots(value):
    shift = SLOT
    while shift < LANES:
        value = value + lane_roll(value, shift)
        shift *= 2
    return value


def ends_of(first, last, lane):
    return jnp.where(lane < HALO, first, jnp.where(lane >= LANES - HALO, last, 0.0))


def added(total, term):
    return term if total is None else total + term


def patch(main, edge, width, slot=0):
    size = main.shape[-1]
    first = lane_roll(edge, -(slot * SLOT + HALO))
    last = lane_roll(edge, -(slot * SLOT + 3 * HALO))
    lane = lane_index(main.shape)
    out = jnp.where(lane < width, widen(first, main), main)
    return jnp.where(lane >= size - width, widen(last, main), out)


def pack_kernel(
    members_hbm, innovations_hbm, precision_hbm, counts_hbm,
    low_ref, high_ref, low_message_ref, high_message_ref,
    members_ref, innovations_ref, precision_ref, counts_ref, sems,
):
    copies = [
        pltpu.make_async_copy(source, target, sems.at[i])
        for i, (source, target) in enumerate(
            (
                (members_hbm, members_ref),
                (innovations_hbm, innovations_ref),
                (precision_hbm, precision_ref),
                (counts_hbm, counts_ref),
            )
        )
    ]
    for copy in copies:
        copy.start()
    for copy in copies[1:]:
        copy.wait()
    weight = counts_ref[...].astype(F32) * precision_ref[...]
    fields = (weight * innovations_ref[...], weight)
    copies[0].wait()
    count, levels, size = members_ref.shape
    lane = lane_index((levels, LANES))
    at = lane % SLOT
    low_message, high_message = [None] * low_message_ref.shape[0], [None] * low_message_ref.shape[0]
    for tile in range(low_ref.shape[0]):
        low = high = None
        for slot in range(SLOTS):
            m = tile * SLOTS + slot
            if m < count:
                first, last = members_ref[m, :, :LANES].astype(F32), members_ref[m, :, size - LANES :].astype(F32)
            elif m < count + 2:
                first, last = fields[m - count][:, :LANES], fields[m - count][:, size - LANES :]
            else:
                continue
            ends = ends_of(first, last, lane)
            low = added(low, lane_roll(ends, slot * SLOT + HALO))
            high = added(high, lane_roll(ends, slot * SLOT + 3 * HALO))
        low_ref[tile] = low
        high_ref[tile] = high
        place, shift = divmod(tile, SLOT // HALO)
        low_message[place] = added(low_message[place], lane_roll(jnp.where(at < HALO, low, 0.0), shift * HALO))
        high = lane_roll(jnp.where(at >= 3 * HALO, high, 0.0), shift * HALO - 3 * HALO)
        high_message[place] = added(high_message[place], high)
    for place in range(low_message_ref.shape[0]):
        low_message_ref[place] = low_message[place]
        high_message_ref[place] = high_message[place]


def main_kernel(
    diffusivity_hbm, map_ref, members_ref, innovations_ref, precision_ref, counts_hbm,
    taps_ref, square_ref, adjoint_ref, source_ref, weight_ref, out_ref, x_ref, y_ref,
    diffusivity_ref, counts_ref, sems,
):
    copies = [
        pltpu.make_async_copy(diffusivity_hbm, diffusivity_ref, sems.at[0]),
        pltpu.make_async_copy(counts_hbm, counts_ref, sems.at[1]),
    ]
    for copy in copies:
        copy.start()
    levels = members_ref.shape[1]
    matrix = map_ref[...]
    dims = (((1,), (1,)), ((), ()))
    square = lax.dot_general(matrix, matrix, dims, precision=HIGHEST, preferred_element_type=F32)
    turned = matrix.T
    for k in range(levels):
        square_ref[k] = jnp.broadcast_to(square[:, k : k + 1], (levels, LANES))
        adjoint_ref[k] = jnp.broadcast_to(turned[:, k : k + 1], (levels, LANES))
    for copy in copies:
        copy.wait()
    coef = level_column(diffusivity_ref[...])
    keep = 1.0 - 2.0 * coef
    taps_ref[0] = keep * keep + 2.0 * coef * coef
    taps_ref[1] = 2.0 * keep * coef
    taps_ref[2] = coef * coef
    weight = counts_ref[...].astype(F32) * precision_ref[...]
    source = weight * innovations_ref[...]
    source_ref[...], weight_ref[...] = source, weight
    (out_ref[...],) = apply_ensemble([(members_ref, source)], taps_ref, square_ref, [(x_ref, y_ref)])


def edge_kernel(
    count, low_ref, high_ref, before_ref, after_ref, taps_ref, square_ref, main_ref,
    edge_members_ref, edge_source_ref, edge_weight_ref, out_ref, x_ref, y_ref,
):
    tiles, levels, _ = low_ref.shape
    size = main_ref.shape[1]
    lane = lane_index((levels, LANES))
    at, slot_of = lane % SLOT, lane // SLOT
    for tile in range(tiles):
        place, shift = divmod(tile, SLOT // HALO)
        before = lane_roll(before_ref[place], -shift * HALO)
        after = lane_roll(after_ref[place], (3 - shift) * HALO)
        own = jnp.where(at >= 2 * HALO, high_ref[tile], low_ref[tile])
        value = jnp.where(at >= 3 * HALO, after, jnp.where(at < HALO, before, own))
        for i, field_ref in enumerate((edge_source_ref, edge_weight_ref)):
            place, slot = divmod(count + i, SLOTS)
            if place == tile:
                field_ref[...] = all_slots(jnp.where(slot_of == slot, value, 0.0))
        held = min(max(count - tile * SLOTS, 0), SLOTS)
        edge_members_ref[tile] = value if held == SLOTS else jnp.where(slot_of < held, value, 0.0)
    (edge,) = apply_ensemble([(edge_members_ref, edge_source_ref[...])], taps_ref, square_ref, [(x_ref, y_ref)])
    edge = all_slots(edge)
    out_ref[:, :size] = patch(main_ref[...], edge, REACH)
    out_ref[:, size:] = edge


def tree_sum(own_ref, a_ref, b_ref, c_ref):
    return (own_ref[...] + a_ref[...]) + (b_ref[...] + c_ref[...])


def second_kernel(
    members_ref, edge_members_ref, weight_ref, edge_weight_ref, taps_ref, square_ref, own_ref, a_ref, b_ref, c_ref, _,
    first_ref, weighted_ref, edge_weighted_ref, out_ref, x_ref, y_ref, edge_x_ref, edge_y_ref,
):
    _, levels, size = members_ref.shape
    lane = lane_index((levels, LANES))
    at = lane % SLOT
    total = tree_sum(own_ref, a_ref, b_ref, c_ref)
    first, edge = total[:, :size], total[:, size:]
    ends = ends_of(first[:, :LANES], first[:, size - LANES :], lane)
    own = jnp.where(lane >= 2 * HALO, lane_roll(ends, 3 * HALO), lane_roll(ends, HALO))
    own = all_slots(jnp.where(lane < SLOT, own, 0.0))
    edge = jnp.where((at >= HALO) & (at < 3 * HALO), own, edge)
    weighted = weight_ref[...] * first
    edge_weighted = edge_weight_ref[...] * edge
    first_ref[...] = first
    weighted_ref[...] = weighted
    edge_weighted_ref[...] = edge_weighted
    main, edge = apply_ensemble(
        [(members_ref, weighted), (edge_members_ref, edge_weighted)], taps_ref, square_ref,
        [(x_ref, y_ref), (edge_x_ref, edge_y_ref)],
    )
    out_ref[...] = patch(main, all_slots(edge), REACH)


def moments_kernel(
    source_ref, weight_ref, first_ref, weighted_ref, own_ref, a_ref, b_ref, c_ref, _, second_ref, moments_ref
):
    size = first_ref.shape[1]
    source, weight = source_ref[...], weight_ref[...]
    first, weighted = first_ref[...], weighted_ref[...]
    second = tree_sum(own_ref, a_ref, b_ref, c_ref)
    second_ref[...] = second
    lane = lane_index((1, LANES))
    width = LANES // 4
    out = jnp.zeros((1, LANES), F32)
    for i, product in enumerate((source * first, weighted * first, weighted * second, weight * second * second)):
        row = sum(product[:, at : at + LANES] for at in range(0, size, LANES))
        row = jnp.sum(row, axis=0, keepdims=True)
        row = row + lane_roll(row, LANES // 2)
        row = row + lane_roll(row, LANES // 4)
        out = jnp.where((lane >= i * width) & (lane < (i + 1) * width), row, out)
    moments_ref[...] = out


def adjoint_kernel(
    members_ref, edge_members_ref, field_ref, edge_field_ref, taps_ref, adjoint_ref, out_ref, x_ref, edge_x_ref
):
    field, edge_field = field_ref[...], edge_field_ref[...]
    taps, edge_taps = wide_taps(taps_ref, field), wide_taps(taps_ref, edge_field)
    for tile in range(edge_members_ref.shape[0]):
        edge_x_ref[tile] = smooth(edge_members_ref[tile] * edge_field, edge_taps)
    for m in range(members_ref.shape[0]):
        main = smooth(members_ref[m].astype(F32) * field, taps)
        x_ref[m] = patch(main, edge_x_ref[m // SLOTS], DIFF, m % SLOTS)
    for m in range(members_ref.shape[0]):
        out_ref[m] = mixed(adjoint_ref, x_ref.at[m])


def final_kernel(
    own_ref, a_ref, b_ref, c_ref, start_ref, image_ref, first_ref, second_ref, control_ref, increment_ref
):
    lane = lane_index((1, LANES))
    width = LANES // 4
    row = tree_sum(own_ref, a_ref, b_ref, c_ref)
    sums = [
        jnp.sum(jnp.where((lane >= i * width) & (lane < (i + 1) * width), row, 0.0), axis=1, keepdims=True)
        for i in range(4)
    ]
    m1, m2, m3 = (value / sums[0] for value in sums[1:])
    alpha = 1.0 / (1.0 + m1)
    spread = jnp.maximum(m2 - m1 * m1, 0.0)
    bend = jnp.maximum(m3 - 2.0 * m1 * m2 + m1 * m1 * m1, 0.0)
    beta = alpha * alpha * spread
    below = spread + bend - alpha * spread * spread
    usable = (spread > 0.0) & (below > 0.0)
    later = jnp.where(usable, jnp.minimum(spread / jnp.where(usable, below, 1.0), 1.0), 0.0)
    on_start = alpha + later * (alpha * m1 + beta)
    on_image = -later * alpha
    increment_ref[...] = on_start * first_ref[...] + on_image * second_ref[...]
    for m in range(start_ref.shape[0]):
        control_ref[m] = on_start * start_ref[m] + on_image * image_ref[m]


def vmem():
    return pl.BlockSpec(memory_space=pltpu.VMEM)


def elsewhere():
    return pl.BlockSpec(memory_space=pl.ANY)


def call(kernel, name, outs, args, scratch=(), specs=None, flops=0, limit=VMEM_LIMIT):
    specs = specs or {}
    moved = sum(a.size * a.dtype.itemsize for a in (*args, *outs))
    return pl.pallas_call(
        kernel,
        name=name,
        out_shape=list(outs),
        in_specs=[specs.get(i, vmem)() for i in range(len(args))],
        out_specs=[vmem()] * len(outs),
        scratch_shapes=list(scratch),
        cost_estimate=pl.CostEstimate(flops=flops, bytes_accessed=moved, transcendentals=0),
        compiler_params=pltpu.CompilerParams(vmem_limit_bytes=limit),
    )(*args)


def shape_of(*dims, dtype=F32):
    return jax.ShapeDtypeStruct(dims, dtype)


def from_partners(value, axis):
    size = lax.axis_size(axis)
    return [lax.ppermute(value, axis, [(i, i ^ step) for i in range(size)]) for step in range(1, size)]


def partner(value, axis, step):
    return lax.ppermute(value, axis, [(i, i ^ step) for i in range(lax.axis_size(axis))])


def domain_terms(value, axis):
    size = lax.axis_size(axis)
    value, step = value + partner(value, axis, 1), 2
    while 4 * step < size:
        if (size // step).bit_length() % 2:
            terms = [partner(value, axis, (k * step) ^ 1) for k in (1, 2, 3)]
            value, step = (value + terms[0]) + (terms[1] + terms[2]), 4 * step
        else:
            value, step = value + partner(value, axis, step ^ 1), 2 * step
    return [value, *(partner(value, axis, (k * step) ^ 1) for k in (1, 2, 3))]


def local(perturbations, innovations, precision_field, obs_counts, vertical_map, diffusivity):
    count, levels, size = perturbations.shape
    tiles = -(-(count + 2) // SLOTS)
    domains = lax.axis_size("domain")
    up = [(i, (i + 1) % domains) for i in range(domains)]
    down = [(j, i) for i, j in up]
    level = shape_of(levels, size)
    members_f32 = shape_of(count, levels, size)
    edge_tiles = shape_of(tiles, levels, LANES)
    edge_row = shape_of(1, LANES)
    edge_level = shape_of(levels, LANES)
    message = shape_of(-(-tiles * HALO // SLOT), levels, LANES)
    column = shape_of(levels, levels, LANES)
    work, edge_work = count * levels * size * 50, tiles * levels * LANES * 50
    scratch = [pltpu.VMEM((count, levels, size), F32)] * 2
    edge_scratch = [pltpu.VMEM((tiles, levels, LANES), F32)] * 2

    counts = obs_counts.reshape(1, size)
    low, high, low_message, high_message = call(
        pack_kernel, "pack_edges", [edge_tiles, edge_tiles, message, message],
        (perturbations, innovations, precision_field, counts),
        [
            pltpu.VMEM((count, levels, size), perturbations.dtype), pltpu.VMEM((levels, size), F32),
            pltpu.VMEM((levels, size), F32), pltpu.VMEM((1, size), jnp.int32), pltpu.SemaphoreType.DMA((4,)),
        ],
        dict.fromkeys(range(4), elsewhere), tiles * levels * LANES * 20, None,
    )
    before = lax.ppermute(low_message, "domain", up)
    after = lax.ppermute(high_message, "domain", down)
    taps, square, mapped, source, weight, main = call(
        main_kernel, "first_inner", [shape_of(3, levels, LANES), column, column, level, level, level],
        (diffusivity.reshape(1, levels), vertical_map, perturbations, innovations, precision_field, counts),
        scratch + [pltpu.VMEM((1, levels), F32), pltpu.VMEM((1, size), jnp.int32), pltpu.SemaphoreType.DMA((2,))],
        {0: elsewhere, 5: elsewhere}, work,
    )
    edge_members, edge_source, edge_weight, part = call(
        functools.partial(edge_kernel, count), "first_edges",
        [edge_tiles, edge_level, edge_level, shape_of(levels, size + LANES)],
        (low, high, before, after, taps, square, main), edge_scratch, flops=edge_work,
    )

    def adjoint(name, field, edge_field):
        (out,) = call(
            adjoint_kernel, name, [members_f32], (perturbations, edge_members, field, edge_field, taps, mapped),
            [scratch[0], edge_scratch[0]], flops=work,
        )
        return out

    others = from_partners(part, "member")
    start = adjoint("start_vector", source, edge_source)
    first, weighted, edge_weighted, part = call(
        second_kernel, "second_apply", [level, level, edge_level, level],
        (perturbations, edge_members, weight, edge_weight, taps, square, part, *others, start),
        scratch + edge_scratch, {10: elsewhere}, work + edge_work,
    )
    others = from_partners(part, "member")
    image = adjoint("image_vector", weighted, edge_weighted)
    second, moments = call(
        moments_kernel, "moments", [level, edge_row],
        (source, weight, first, weighted, part, *others, image), (), {8: elsewhere},
    )
    moments = domain_terms(moments, "domain")
    return tuple(
        call(final_kernel, "combine", [members_f32, level], (*moments, start, image, first, second))
    )


def solution(mesh):
    in_specs = (
        P("member", None, "domain"),
        P(None, "domain"),
        P(None, "domain"),
        P("domain"),
        P(),
        P(),
    )
    out_specs = (P("member", None, "domain"), P(None, "domain"))
    return jax.shard_map(local, mesh=mesh, in_specs=in_specs, out_specs=out_specs, check_vma=False)
```

```python
import functools

import jax
import jax.numpy as jnp
from jax import lax
from jax.experimental import pallas as pl
from jax.experimental.pallas import tpu as pltpu
from jax.sharding import PartitionSpec as P

DIFF = 2
LANES = 128
REACH = 2 * DIFF
HALO = 2 * REACH
SLOT = 4 * HALO
SLOTS = LANES // SLOT
SHIFTS = range(-DIFF, DIFF + 1)
F32 = jnp.float32
HIGHEST = lax.Precision.HIGHEST
VMEM_LIMIT = 32 * 1024 * 1024


def lane_roll(value, shift):
    return pltpu.roll(value, shift % value.shape[-1], value.ndim - 1)


def lane_index(shape):
    return lax.broadcasted_iota(jnp.int32, shape, len(shape) - 1)


def widen(column, like):
    copies = like.shape[-1] // LANES
    return column if copies == 1 else jnp.concatenate([column] * copies, axis=-1)


def level_column(row):
    levels = row.shape[1]
    square = jnp.broadcast_to(row, (levels, levels))
    own = lax.broadcasted_iota(jnp.int32, square.shape, 0) == lane_index(square.shape)
    return jnp.broadcast_to(jnp.sum(jnp.where(own, square, 0.0), axis=1, keepdims=True), (levels, LANES))


def smooth(field, taps):
    near = lane_roll(field, 1) + lane_roll(field, -1)
    far = lane_roll(field, 2) + lane_roll(field, -2)
    return taps[0] * field + taps[1] * near + taps[2] * far


def mixed(mix_ref, field_ref):
    out = None
    for k in range(mix_ref.shape[0]):
        row = field_ref[k : k + 1, :]
        term = widen(mix_ref[k], row) * row
        out = term if out is None else out + term
    return out


def wide_taps(taps_ref, like):
    return [widen(taps_ref[i], like) for i in range(3)]


def shifted_by(value, shift):
    return value if shift == 0 else lane_roll(value, shift)


def smooth_product(shifted_ref, m, steps):
    out = None
    for i, step in enumerate(steps):
        term = shifted_ref[i, m].astype(F32) * step
        out = term if out is None else out + term
    return out


def field_steps(field, taps_ref):
    taps = wide_taps(taps_ref, field)
    return [taps[abs(s)] * shifted_by(field, s) for s in SHIFTS]


def apply_shifted(shifted_ref, field, taps_ref, blocks_ref, split_ref, y_ref):
    _, count, levels, size = shifted_ref.shape
    rows = blocks_ref.shape[0]
    group = rows // levels
    steps = field_steps(field, taps_ref)
    for m in range(count):
        value = smooth_product(shifted_ref, m, steps)
        high = value.astype(jnp.bfloat16)
        low = (value - high.astype(F32)).astype(jnp.bfloat16)
        place, at = m // group, m % group * levels
        for base, part in ((0, high), (rows, high), (2 * rows, low)):
            split_ref[place, base + at : base + at + levels] = part
    for place in range(count // group):
        value = jnp.dot(blocks_ref[...], split_ref[place], preferred_element_type=F32)
        y_ref[place * group : (place + 1) * group] = value.reshape(group, levels, size)
    totals = [jnp.zeros((levels, size), F32)] * len(SHIFTS)
    for m in range(count):
        value = y_ref[m]
        totals = [total + shifted_ref[i, m].astype(F32) * value for i, total in enumerate(totals)]
    taps = wide_taps(taps_ref, field)
    return sum(taps[abs(s)] * shifted_by(total, -s) for s, total in zip(SHIFTS, totals))


def apply_ensemble(parts, taps_ref, mix_ref, scratches):
    totals = []
    for (members_ref, field), (x_ref, y_ref) in zip(parts, scratches):
        taps = wide_taps(taps_ref, field)
        for m in range(members_ref.shape[0]):
            x_ref[m] = smooth(members_ref[m].astype(F32) * field, taps)
    for (members_ref, field), (x_ref, y_ref) in zip(parts, scratches):
        for m in range(members_ref.shape[0]):
            y_ref[m] = mixed(mix_ref, x_ref.at[m])
    for (members_ref, field), (x_ref, y_ref) in zip(parts, scratches):
        taps = wide_taps(taps_ref, field)
        total = jnp.zeros(field.shape, F32)
        for m in range(members_ref.shape[0]):
            total = total + members_ref[m].astype(F32) * smooth(y_ref[m], taps)
        totals.append(total)
    return totals


def all_slots(value):
    shift = SLOT
    while shift < LANES:
        value = value + lane_roll(value, shift)
        shift *= 2
    return value


def ends_of(first, last, lane):
    return jnp.where(lane < HALO, first, jnp.where(lane >= LANES - HALO, last, 0.0))


def added(total, term):
    return term if total is None else total + term


def patch(main, edge, width, slot=0):
    size = main.shape[-1]
    first = lane_roll(edge, -(slot * SLOT + HALO))
    last = lane_roll(edge, -(slot * SLOT + 3 * HALO))
    lane = lane_index(main.shape)
    out = jnp.where(lane < width, widen(first, main), main)
    return jnp.where(lane >= size - width, widen(last, main), out)


def pack_kernel(
    members_hbm, innovations_hbm, precision_hbm, counts_hbm,
    low_ref, high_ref, low_message_ref, high_message_ref,
    members_ref, innovations_ref, precision_ref, counts_ref, sems,
):
    copies = [
        pltpu.make_async_copy(source, target, sems.at[i])
        for i, (source, target) in enumerate(
            (
                (members_hbm, members_ref),
                (innovations_hbm, innovations_ref),
                (precision_hbm, precision_ref),
                (counts_hbm, counts_ref),
            )
        )
    ]
    for copy in copies:
        copy.start()
    for copy in copies[1:]:
        copy.wait()
    weight = counts_ref[...].astype(F32) * precision_ref[...]
    fields = (weight * innovations_ref[...], weight)
    copies[0].wait()
    count, levels, size = members_ref.shape
    lane = lane_index((levels, LANES))
    at = lane % SLOT
    low_message, high_message = [None] * low_message_ref.shape[0], [None] * low_message_ref.shape[0]
    for tile in range(low_ref.shape[0]):
        low = high = None
        for slot in range(SLOTS):
            m = tile * SLOTS + slot
            if m < count:
                first, last = members_ref[m, :, :LANES].astype(F32), members_ref[m, :, size - LANES :].astype(F32)
            elif m < count + 2:
                first, last = fields[m - count][:, :LANES], fields[m - count][:, size - LANES :]
            else:
                continue
            ends = ends_of(first, last, lane)
            low = added(low, lane_roll(ends, slot * SLOT + HALO))
            high = added(high, lane_roll(ends, slot * SLOT + 3 * HALO))
        low_ref[tile] = low
        high_ref[tile] = high
        place, shift = divmod(tile, SLOT // HALO)
        low_message[place] = added(low_message[place], lane_roll(jnp.where(at < HALO, low, 0.0), shift * HALO))
        high = lane_roll(jnp.where(at >= 3 * HALO, high, 0.0), shift * HALO - 3 * HALO)
        high_message[place] = added(high_message[place], high)
    for place in range(low_message_ref.shape[0]):
        low_message_ref[place] = low_message[place]
        high_message_ref[place] = high_message[place]


def main_kernel(
    diffusivity_hbm, map_ref, members_ref, innovations_ref, precision_ref, counts_hbm,
    taps_ref, square_ref, adjoint_ref, blocks_ref, shifted_ref, source_ref, weight_ref, out_ref,
    split_ref, y_ref, diffusivity_ref, counts_ref, sems,
):
    copies = [
        pltpu.make_async_copy(diffusivity_hbm, diffusivity_ref, sems.at[0]),
        pltpu.make_async_copy(counts_hbm, counts_ref, sems.at[1]),
    ]
    for copy in copies:
        copy.start()
    levels = members_ref.shape[1]
    matrix = map_ref[...]
    dims = (((1,), (1,)), ((), ()))
    square = lax.dot_general(matrix, matrix, dims, precision=HIGHEST, preferred_element_type=F32)
    turned = matrix.T
    rows, width = blocks_ref.shape
    column = lane_index((levels, -(-width // LANES) * LANES))
    block = jnp.zeros(column.shape, F32)
    for k in range(levels):
        square_ref[k] = jnp.broadcast_to(square[:, k : k + 1], (levels, LANES))
        block = jnp.where(column % levels == k, widen(square_ref[k], block), block)
        adjoint_ref[k] = jnp.broadcast_to(turned[:, k : k + 1], (levels, LANES))
    high = block.astype(jnp.bfloat16).astype(F32)
    block = jnp.where(column // rows == 1, block - high, high)
    for i in range(rows // levels):
        value = jnp.where(column % rows // levels == i, block, 0.0).astype(jnp.bfloat16)
        blocks_ref[i * levels : (i + 1) * levels] = value[:, :width]
    for m in range(members_ref.shape[0]):
        value = members_ref[m].astype(F32)
        for i, s in enumerate(SHIFTS):
            shifted_ref[i, m] = shifted_by(value, s).astype(shifted_ref.dtype)
    for copy in copies:
        copy.wait()
    coef = level_column(diffusivity_ref[...])
    keep = 1.0 - 2.0 * coef
    taps_ref[0] = keep * keep + 2.0 * coef * coef
    taps_ref[1] = 2.0 * keep * coef
    taps_ref[2] = coef * coef
    weight = counts_ref[...].astype(F32) * precision_ref[...]
    source = weight * innovations_ref[...]
    source_ref[...], weight_ref[...] = source, weight
    out_ref[...] = apply_shifted(shifted_ref, source, taps_ref, blocks_ref, split_ref, y_ref)


def edge_kernel(
    count, low_ref, high_ref, before_ref, after_ref, taps_ref, square_ref, main_ref,
    edge_members_ref, edge_source_ref, edge_weight_ref, out_ref, x_ref, y_ref,
):
    tiles, levels, _ = low_ref.shape
    size = main_ref.shape[1]
    lane = lane_index((levels, LANES))
    at, slot_of = lane % SLOT, lane // SLOT
    for tile in range(tiles):
        place, shift = divmod(tile, SLOT // HALO)
        before = lane_roll(before_ref[place], -shift * HALO)
        after = lane_roll(after_ref[place], (3 - shift) * HALO)
        own = jnp.where(at >= 2 * HALO, high_ref[tile], low_ref[tile])
        value = jnp.where(at >= 3 * HALO, after, jnp.where(at < HALO, before, own))
        for i, field_ref in enumerate((edge_source_ref, edge_weight_ref)):
            place, slot = divmod(count + i, SLOTS)
            if place == tile:
                field_ref[...] = all_slots(jnp.where(slot_of == slot, value, 0.0))
        held = min(max(count - tile * SLOTS, 0), SLOTS)
        edge_members_ref[tile] = value if held == SLOTS else jnp.where(slot_of < held, value, 0.0)
    (edge,) = apply_ensemble([(edge_members_ref, edge_source_ref[...])], taps_ref, square_ref, [(x_ref, y_ref)])
    edge = all_slots(edge)
    out_ref[:, :size] = patch(main_ref[...], edge, REACH)
    out_ref[:, size:] = edge


def tree_sum(own_ref, a_ref, b_ref, c_ref):
    return (own_ref[...] + a_ref[...]) + (b_ref[...] + c_ref[...])


def second_kernel(
    shifted_ref, edge_members_ref, weight_ref, edge_weight_ref, taps_ref, square_ref, blocks_ref,
    own_ref, a_ref, b_ref, c_ref, _,
    first_ref, weighted_ref, edge_weighted_ref, out_ref, split_ref, y_ref, edge_x_ref, edge_y_ref,
):
    levels, size = weight_ref.shape
    lane = lane_index((levels, LANES))
    at = lane % SLOT
    total = tree_sum(own_ref, a_ref, b_ref, c_ref)
    first, edge = total[:, :size], total[:, size:]
    ends = ends_of(first[:, :LANES], first[:, size - LANES :], lane)
    own = jnp.where(lane >= 2 * HALO, lane_roll(ends, 3 * HALO), lane_roll(ends, HALO))
    own = all_slots(jnp.where(lane < SLOT, own, 0.0))
    edge = jnp.where((at >= HALO) & (at < 3 * HALO), own, edge)
    weighted = weight_ref[...] * first
    edge_weighted = edge_weight_ref[...] * edge
    first_ref[...] = first
    weighted_ref[...] = weighted
    edge_weighted_ref[...] = edge_weighted
    main = apply_shifted(shifted_ref, weighted, taps_ref, blocks_ref, split_ref, y_ref)
    (edge,) = apply_ensemble(
        [(edge_members_ref, edge_weighted)], taps_ref, square_ref, [(edge_x_ref, edge_y_ref)]
    )
    out_ref[...] = patch(main, all_slots(edge), REACH)


def moments_kernel(
    source_ref, weight_ref, first_ref, weighted_ref, own_ref, a_ref, b_ref, c_ref, _, second_ref, moments_ref
):
    size = first_ref.shape[1]
    source, weight = source_ref[...], weight_ref[...]
    first, weighted = first_ref[...], weighted_ref[...]
    second = tree_sum(own_ref, a_ref, b_ref, c_ref)
    second_ref[...] = second
    lane = lane_index((1, LANES))
    width = LANES // 4
    out = jnp.zeros((1, LANES), F32)
    for i, product in enumerate((source * first, weighted * first, weighted * second, weight * second * second)):
        row = sum(product[:, at : at + LANES] for at in range(0, size, LANES))
        row = jnp.sum(row, axis=0, keepdims=True)
        row = row + lane_roll(row, LANES // 2)
        row = row + lane_roll(row, LANES // 4)
        out = jnp.where((lane >= i * width) & (lane < (i + 1) * width), row, out)
    moments_ref[...] = out


def adjoint_kernel(
    shifted_ref, edge_members_ref, field_ref, edge_field_ref, taps_ref, adjoint_ref, out_ref, x_ref, edge_x_ref
):
    field, edge_field = field_ref[...], edge_field_ref[...]
    steps, edge_taps = field_steps(field, taps_ref), wide_taps(taps_ref, edge_field)
    for tile in range(edge_members_ref.shape[0]):
        edge_x_ref[tile] = smooth(edge_members_ref[tile] * edge_field, edge_taps)
    for m in range(out_ref.shape[0]):
        main = smooth_product(shifted_ref, m, steps)
        x_ref[m] = patch(main, edge_x_ref[m // SLOTS], DIFF, m % SLOTS)
    for m in range(out_ref.shape[0]):
        out_ref[m] = mixed(adjoint_ref, x_ref.at[m])


def final_kernel(
    own_ref, a_ref, b_ref, c_ref, start_ref, image_ref, first_ref, second_ref, control_ref, increment_ref
):
    lane = lane_index((1, LANES))
    width = LANES // 4
    row = tree_sum(own_ref, a_ref, b_ref, c_ref)
    sums = [
        jnp.sum(jnp.where((lane >= i * width) & (lane < (i + 1) * width), row, 0.0), axis=1, keepdims=True)
        for i in range(4)
    ]
    m1, m2, m3 = (value / sums[0] for value in sums[1:])
    alpha = 1.0 / (1.0 + m1)
    spread = jnp.maximum(m2 - m1 * m1, 0.0)
    bend = jnp.maximum(m3 - 2.0 * m1 * m2 + m1 * m1 * m1, 0.0)
    beta = alpha * alpha * spread
    below = spread + bend - alpha * spread * spread
    usable = (spread > 0.0) & (below > 0.0)
    later = jnp.where(usable, jnp.minimum(spread / jnp.where(usable, below, 1.0), 1.0), 0.0)
    on_start = alpha + later * (alpha * m1 + beta)
    on_image = -later * alpha
    increment_ref[...] = on_start * first_ref[...] + on_image * second_ref[...]
    for m in range(start_ref.shape[0]):
        control_ref[m] = on_start * start_ref[m] + on_image * image_ref[m]


def vmem():
    return pl.BlockSpec(memory_space=pltpu.VMEM)


def elsewhere():
    return pl.BlockSpec(memory_space=pl.ANY)


def call(kernel, name, outs, args, scratch=(), specs=None, flops=0, limit=VMEM_LIMIT):
    specs = specs or {}
    moved = sum(a.size * a.dtype.itemsize for a in (*args, *outs))
    return pl.pallas_call(
        kernel,
        name=name,
        out_shape=list(outs),
        in_specs=[specs.get(i, vmem)() for i in range(len(args))],
        out_specs=[vmem()] * len(outs),
        scratch_shapes=list(scratch),
        cost_estimate=pl.CostEstimate(flops=flops, bytes_accessed=moved, transcendentals=0),
        compiler_params=pltpu.CompilerParams(vmem_limit_bytes=limit),
    )(*args)


def shape_of(*dims, dtype=F32):
    return jax.ShapeDtypeStruct(dims, dtype)


def from_partners(value, axis):
    size = lax.axis_size(axis)
    return [lax.ppermute(value, axis, [(i, i ^ step) for i in range(size)]) for step in range(1, size)]


def partner(value, axis, step):
    return lax.ppermute(value, axis, [(i, i ^ step) for i in range(lax.axis_size(axis))])


def domain_terms(value, axis):
    size = lax.axis_size(axis)
    value, step = value + partner(value, axis, 1), 2
    while 4 * step < size:
        if (size // step).bit_length() % 2:
            terms = [partner(value, axis, (k * step) ^ 1) for k in (1, 2, 3)]
            value, step = (value + terms[0]) + (terms[1] + terms[2]), 4 * step
        else:
            value, step = value + partner(value, axis, step ^ 1), 2 * step
    return [value, *(partner(value, axis, (k * step) ^ 1) for k in (1, 2, 3))]


def local(perturbations, innovations, precision_field, obs_counts, vertical_map, diffusivity):
    count, levels, size = perturbations.shape
    tiles = -(-(count + 2) // SLOTS)
    domains = lax.axis_size("domain")
    up = [(i, (i + 1) % domains) for i in range(domains)]
    down = [(j, i) for i, j in up]
    level = shape_of(levels, size)
    members_f32 = shape_of(count, levels, size)
    edge_tiles = shape_of(tiles, levels, LANES)
    edge_row = shape_of(1, LANES)
    edge_level = shape_of(levels, LANES)
    message = shape_of(-(-tiles * HALO // SLOT), levels, LANES)
    column = shape_of(levels, levels, LANES)
    work, edge_work = count * levels * size * 50, tiles * levels * LANES * 50
    scratch = [pltpu.VMEM((count, levels, size), F32)] * 2
    edge_scratch = [pltpu.VMEM((tiles, levels, LANES), F32)] * 2

    counts = obs_counts.reshape(1, size)
    low, high, low_message, high_message = call(
        pack_kernel, "pack_edges", [edge_tiles, edge_tiles, message, message],
        (perturbations, innovations, precision_field, counts),
        [
            pltpu.VMEM((count, levels, size), perturbations.dtype), pltpu.VMEM((levels, size), F32),
            pltpu.VMEM((levels, size), F32), pltpu.VMEM((1, size), jnp.int32), pltpu.SemaphoreType.DMA((4,)),
        ],
        dict.fromkeys(range(4), elsewhere), tiles * levels * LANES * 20, None,
    )
    before = lax.ppermute(low_message, "domain", up)
    after = lax.ppermute(high_message, "domain", down)
    group = max(g for g in range(1, 6) if count % g == 0)
    blocks = shape_of(group * levels, 3 * group * levels, dtype=jnp.bfloat16)
    split = pltpu.VMEM((count // group, 3 * group * levels, size), jnp.bfloat16)
    taps, square, mapped, blocks, shifted, source, weight, main = call(
        main_kernel, "first_inner",
        [
            shape_of(3, levels, LANES), column, column, blocks, shape_of(len(SHIFTS), count, levels, size, dtype=perturbations.dtype),
            level, level, level,
        ],
        (diffusivity.reshape(1, levels), vertical_map, perturbations, innovations, precision_field, counts),
        [split, scratch[0], pltpu.VMEM((1, levels), F32), pltpu.VMEM((1, size), jnp.int32), pltpu.SemaphoreType.DMA((2,))],
        {0: elsewhere, 5: elsewhere}, work,
    )
    edge_members, edge_source, edge_weight, part = call(
        functools.partial(edge_kernel, count), "first_edges",
        [edge_tiles, edge_level, edge_level, shape_of(levels, size + LANES)],
        (low, high, before, after, taps, square, main), edge_scratch, flops=edge_work,
    )

    def adjoint(name, field, edge_field):
        (out,) = call(
            adjoint_kernel, name, [members_f32], (shifted, edge_members, field, edge_field, taps, mapped),
            [scratch[0], edge_scratch[0]], flops=work,
        )
        return out

    others = from_partners(part, "member")
    start = adjoint("start_vector", source, edge_source)
    first, weighted, edge_weighted, part = call(
        second_kernel, "second_apply", [level, level, edge_level, level],
        (shifted, edge_members, weight, edge_weight, taps, square, blocks, part, *others, start),
        [split, scratch[0], *edge_scratch], {11: elsewhere}, work + edge_work,
    )
    others = from_partners(part, "member")
    image = adjoint("image_vector", weighted, edge_weighted)
    second, moments = call(
        moments_kernel, "moments", [level, edge_row],
        (source, weight, first, weighted, part, *others, image), (), {8: elsewhere},
    )
    moments = domain_terms(moments, "domain")
    return tuple(
        call(final_kernel, "combine", [members_f32, level], (*moments, start, image, first, second))
    )


def solution(mesh):
    in_specs = (
        P("member", None, "domain"),
        P(None, "domain"),
        P(None, "domain"),
        P("domain"),
        P(),
        P(),
    )
    out_specs = (P("member", None, "domain"), P(None, "domain"))
    return jax.shard_map(local, mesh=mesh, in_specs=in_specs, out_specs=out_specs, check_vma=False)
```

```python
import functools

import jax
import jax.numpy as jnp
from jax import lax
from jax.experimental import pallas as pl
from jax.experimental.pallas import tpu as pltpu
from jax.sharding import PartitionSpec as P

DIFF = 2
LANES = 128
REACH = 2 * DIFF
HALO = 2 * REACH
SLOT = 4 * HALO
SLOTS = LANES // SLOT
SHIFTS = range(-DIFF, DIFF + 1)
F32 = jnp.float32
HIGHEST = lax.Precision.HIGHEST
VMEM_LIMIT = 32 * 1024 * 1024


def lane_roll(value, shift):
    return pltpu.roll(value, shift % value.shape[-1], value.ndim - 1)


def lane_index(shape):
    return lax.broadcasted_iota(jnp.int32, shape, len(shape) - 1)


def widen(column, like):
    copies = like.shape[-1] // LANES
    return column if copies == 1 else jnp.concatenate([column] * copies, axis=-1)


def level_column(row):
    levels = row.shape[1]
    square = jnp.broadcast_to(row, (levels, levels))
    own = lax.broadcasted_iota(jnp.int32, square.shape, 0) == lane_index(square.shape)
    return jnp.broadcast_to(jnp.sum(jnp.where(own, square, 0.0), axis=1, keepdims=True), (levels, LANES))


def smooth(field, taps):
    near = lane_roll(field, 1) + lane_roll(field, -1)
    far = lane_roll(field, 2) + lane_roll(field, -2)
    return taps[0] * field + taps[1] * near + taps[2] * far


def mixed(mix_ref, field_ref):
    out = None
    for k in range(mix_ref.shape[0]):
        row = field_ref[k : k + 1, :]
        term = widen(mix_ref[k], row) * row
        out = term if out is None else out + term
    return out


def wide_taps(taps_ref, like):
    return [widen(taps_ref[i], like) for i in range(3)]


def shifted_by(value, shift):
    return value if shift == 0 else lane_roll(value, shift)


def smooth_product(shifted_ref, m, steps):
    out = None
    for i, step in enumerate(steps):
        term = shifted_ref[i, m].astype(F32) * step
        out = term if out is None else out + term
    return out


def field_steps(field, taps_ref):
    taps = wide_taps(taps_ref, field)
    return [taps[abs(s)] * shifted_by(field, s) for s in SHIFTS]


def apply_shifted(shifted_ref, field, taps_ref, blocks_ref, split_ref, y_ref):
    _, count, levels, size = shifted_ref.shape
    rows = blocks_ref.shape[0]
    group = rows // levels
    steps = field_steps(field, taps_ref)
    for m in range(count):
        value = smooth_product(shifted_ref, m, steps)
        high = value.astype(jnp.bfloat16)
        low = (value - high.astype(F32)).astype(jnp.bfloat16)
        place, at = m // group, m % group * levels
        for base, part in ((0, high), (rows, high), (2 * rows, low)):
            split_ref[place, base + at : base + at + levels] = part
    for place in range(count // group):
        value = jnp.dot(blocks_ref[...], split_ref[place], preferred_element_type=F32)
        y_ref[place * group : (place + 1) * group] = value.reshape(group, levels, size)
    totals = [jnp.zeros((levels, size), F32)] * len(SHIFTS)
    for m in range(count):
        value = y_ref[m]
        totals = [total + shifted_ref[i, m].astype(F32) * value for i, total in enumerate(totals)]
    taps = wide_taps(taps_ref, field)
    return sum(taps[abs(s)] * shifted_by(total, -s) for s, total in zip(SHIFTS, totals))


def apply_ensemble(parts, taps_ref, mix_ref, scratches):
    totals = []
    for (members_ref, field), (x_ref, y_ref) in zip(parts, scratches):
        taps = wide_taps(taps_ref, field)
        for m in range(members_ref.shape[0]):
            x_ref[m] = smooth(members_ref[m].astype(F32) * field, taps)
    for (members_ref, field), (x_ref, y_ref) in zip(parts, scratches):
        for m in range(members_ref.shape[0]):
            y_ref[m] = mixed(mix_ref, x_ref.at[m])
    for (members_ref, field), (x_ref, y_ref) in zip(parts, scratches):
        taps = wide_taps(taps_ref, field)
        total = jnp.zeros(field.shape, F32)
        for m in range(members_ref.shape[0]):
            total = total + members_ref[m].astype(F32) * smooth(y_ref[m], taps)
        totals.append(total)
    return totals


def all_slots(value):
    one, two, three = (lane_roll(value, k * SLOT) for k in (1, 2, 3))
    return (value + two) + (one + three)


def ends_of(first, last, lane):
    return jnp.where(lane < HALO, first, jnp.where(lane >= LANES - HALO, last, 0.0))


def added(total, term):
    return term if total is None else total + term


def patch(main, edge, width, slot=0):
    size = main.shape[-1]
    first = lane_roll(edge, -(slot * SLOT + HALO))
    last = lane_roll(edge, -(slot * SLOT + 3 * HALO))
    lane = lane_index(main.shape)
    out = jnp.where(lane < width, widen(first, main), main)
    return jnp.where(lane >= size - width, widen(last, main), out)


def pack_kernel(
    members_hbm, innovations_hbm, precision_hbm, counts_hbm,
    low_ref, high_ref, low_message_ref, high_message_ref,
    members_ref, innovations_ref, precision_ref, counts_ref, sems,
):
    copies = [
        pltpu.make_async_copy(source, target, sems.at[i])
        for i, (source, target) in enumerate(
            (
                (members_hbm, members_ref),
                (innovations_hbm, innovations_ref),
                (precision_hbm, precision_ref),
                (counts_hbm, counts_ref),
            )
        )
    ]
    for copy in copies:
        copy.start()
    for copy in copies[1:]:
        copy.wait()
    weight = counts_ref[...].astype(F32) * precision_ref[...]
    fields = (weight * innovations_ref[...], weight)
    copies[0].wait()
    count, levels, size = members_ref.shape
    lane = lane_index((levels, LANES))
    at = lane % SLOT
    low_message, high_message = [None] * low_message_ref.shape[0], [None] * low_message_ref.shape[0]
    for tile in range(low_ref.shape[0]):
        low = high = None
        for slot in range(SLOTS):
            m = tile * SLOTS + slot
            if m < count:
                first, last = members_ref[m, :, :LANES].astype(F32), members_ref[m, :, size - LANES :].astype(F32)
            elif m < count + 2:
                first, last = fields[m - count][:, :LANES], fields[m - count][:, size - LANES :]
            else:
                continue
            ends = ends_of(first, last, lane)
            low = added(low, lane_roll(ends, slot * SLOT + HALO))
            high = added(high, lane_roll(ends, slot * SLOT + 3 * HALO))
        low_ref[tile] = low
        high_ref[tile] = high
        place, shift = divmod(tile, SLOT // HALO)
        low_message[place] = added(low_message[place], lane_roll(jnp.where(at < HALO, low, 0.0), shift * HALO))
        high = lane_roll(jnp.where(at >= 3 * HALO, high, 0.0), shift * HALO - 3 * HALO)
        high_message[place] = added(high_message[place], high)
    for place in range(low_message_ref.shape[0]):
        low_message_ref[place] = low_message[place]
        high_message_ref[place] = high_message[place]


def main_kernel(
    diffusivity_hbm, map_ref, members_ref, innovations_ref, precision_ref, counts_hbm,
    taps_ref, square_ref, adjoint_ref, blocks_ref, shifted_ref, source_ref, weight_ref, out_ref,
    split_ref, y_ref, diffusivity_ref, counts_ref, sems,
):
    copies = [
        pltpu.make_async_copy(diffusivity_hbm, diffusivity_ref, sems.at[0]),
        pltpu.make_async_copy(counts_hbm, counts_ref, sems.at[1]),
    ]
    for copy in copies:
        copy.start()
    levels = members_ref.shape[1]
    matrix = map_ref[...]
    dims = (((1,), (1,)), ((), ()))
    square = lax.dot_general(matrix, matrix, dims, precision=HIGHEST, preferred_element_type=F32)
    turned = matrix.T
    rows, width = blocks_ref.shape
    column = lane_index((levels, -(-width // LANES) * LANES))
    block = jnp.zeros(column.shape, F32)
    for k in range(levels):
        square_ref[k] = jnp.broadcast_to(square[:, k : k + 1], (levels, LANES))
        block = jnp.where(column % levels == k, widen(square_ref[k], block), block)
        adjoint_ref[k] = jnp.broadcast_to(turned[:, k : k + 1], (levels, LANES))
    high = block.astype(jnp.bfloat16).astype(F32)
    block = jnp.where(column // rows == 1, block - high, high)
    for i in range(rows // levels):
        value = jnp.where(column % rows // levels == i, block, 0.0).astype(jnp.bfloat16)
        blocks_ref[i * levels : (i + 1) * levels] = value[:, :width]
    for m in range(members_ref.shape[0]):
        value = members_ref[m].astype(F32)
        for i, s in enumerate(SHIFTS):
            shifted_ref[i, m] = shifted_by(value, s).astype(shifted_ref.dtype)
    for copy in copies:
        copy.wait()
    coef = level_column(diffusivity_ref[...])
    keep = 1.0 - 2.0 * coef
    taps_ref[0] = keep * keep + 2.0 * coef * coef
    taps_ref[1] = 2.0 * keep * coef
    taps_ref[2] = coef * coef
    weight = counts_ref[...].astype(F32) * precision_ref[...]
    source = weight * innovations_ref[...]
    source_ref[...], weight_ref[...] = source, weight
    out_ref[...] = apply_shifted(shifted_ref, source, taps_ref, blocks_ref, split_ref, y_ref)


def edge_kernel(
    count, low_ref, high_ref, before_ref, after_ref, taps_ref, square_ref, main_ref,
    edge_members_ref, edge_source_ref, edge_weight_ref, out_ref, x_ref, y_ref,
):
    tiles, levels, _ = low_ref.shape
    size = main_ref.shape[1]
    lane = lane_index((levels, LANES))
    at, slot_of = lane % SLOT, lane // SLOT
    for tile in range(tiles):
        place, shift = divmod(tile, SLOT // HALO)
        before = lane_roll(before_ref[place], -shift * HALO)
        after = lane_roll(after_ref[place], (3 - shift) * HALO)
        own = jnp.where(at >= 2 * HALO, high_ref[tile], low_ref[tile])
        value = jnp.where(at >= 3 * HALO, after, jnp.where(at < HALO, before, own))
        for i, field_ref in enumerate((edge_source_ref, edge_weight_ref)):
            place, slot = divmod(count + i, SLOTS)
            if place == tile:
                field_ref[...] = all_slots(jnp.where(slot_of == slot, value, 0.0))
        held = min(max(count - tile * SLOTS, 0), SLOTS)
        edge_members_ref[tile] = value if held == SLOTS else jnp.where(slot_of < held, value, 0.0)
    (edge,) = apply_ensemble([(edge_members_ref, edge_source_ref[...])], taps_ref, square_ref, [(x_ref, y_ref)])
    edge = all_slots(edge)
    out_ref[:, :size] = patch(main_ref[...], edge, REACH)
    out_ref[:, size:] = edge


def tree_sum(own_ref, a_ref, b_ref, c_ref):
    return (own_ref[...] + a_ref[...]) + (b_ref[...] + c_ref[...])


def second_kernel(
    shifted_ref, edge_members_ref, weight_ref, edge_weight_ref, taps_ref, square_ref, blocks_ref,
    own_ref, a_ref, b_ref, c_ref, _,
    first_ref, weighted_ref, edge_weighted_ref, out_ref, split_ref, y_ref, edge_x_ref, edge_y_ref,
):
    levels, size = weight_ref.shape
    lane = lane_index((levels, LANES))
    at = lane % SLOT
    total = tree_sum(own_ref, a_ref, b_ref, c_ref)
    first, edge = total[:, :size], total[:, size:]
    ends = ends_of(first[:, :LANES], first[:, size - LANES :], lane)
    own = jnp.where(lane >= 2 * HALO, lane_roll(ends, 3 * HALO), lane_roll(ends, HALO))
    own = all_slots(jnp.where(lane < SLOT, own, 0.0))
    edge = jnp.where((at >= HALO) & (at < 3 * HALO), own, edge)
    weighted = weight_ref[...] * first
    edge_weighted = edge_weight_ref[...] * edge
    first_ref[...] = first
    weighted_ref[...] = weighted
    edge_weighted_ref[...] = edge_weighted
    main = apply_shifted(shifted_ref, weighted, taps_ref, blocks_ref, split_ref, y_ref)
    (edge,) = apply_ensemble(
        [(edge_members_ref, edge_weighted)], taps_ref, square_ref, [(edge_x_ref, edge_y_ref)]
    )
    out_ref[...] = patch(main, all_slots(edge), REACH)


def moments_kernel(
    source_ref, weight_ref, first_ref, weighted_ref, own_ref, a_ref, b_ref, c_ref, _, second_ref, moments_ref
):
    size = first_ref.shape[1]
    source, weight = source_ref[...], weight_ref[...]
    first, weighted = first_ref[...], weighted_ref[...]
    second = tree_sum(own_ref, a_ref, b_ref, c_ref)
    second_ref[...] = second
    kind = lax.broadcasted_iota(jnp.int32, moments_ref.shape, 0)
    out = jnp.zeros(moments_ref.shape, F32)
    for i, product in enumerate((source * first, weighted * first, weighted * second, weight * second * second)):
        row = sum(product[:, at : at + LANES] for at in range(0, size, LANES))
        out = jnp.where(kind == i, jnp.sum(row, axis=0, keepdims=True), out)
    moments_ref[...] = out


def adjoint_kernel(
    shifted_ref, edge_members_ref, field_ref, edge_field_ref, taps_ref, adjoint_ref, out_ref, x_ref, edge_x_ref
):
    field, edge_field = field_ref[...], edge_field_ref[...]
    steps, edge_taps = field_steps(field, taps_ref), wide_taps(taps_ref, edge_field)
    for tile in range(edge_members_ref.shape[0]):
        edge_x_ref[tile] = smooth(edge_members_ref[tile] * edge_field, edge_taps)
    for m in range(out_ref.shape[0]):
        main = smooth_product(shifted_ref, m, steps)
        x_ref[m] = patch(main, edge_x_ref[m // SLOTS], DIFF, m % SLOTS)
    for m in range(out_ref.shape[0]):
        out_ref[m] = mixed(adjoint_ref, x_ref.at[m])


def final_kernel(
    own_ref, a_ref, b_ref, c_ref, start_ref, image_ref, first_ref, second_ref, control_ref, increment_ref
):
    total = tree_sum(own_ref, a_ref, b_ref, c_ref)
    total = jnp.broadcast_to(jnp.sum(total, axis=1, keepdims=True), total.shape)
    mu = [total[i : i + 1, :] for i in range(4)]
    alpha = mu[0] / (mu[0] + mu[1])
    scale = 1.0 / mu[0]
    m1, m2, m3 = (value * scale for value in mu[1:])
    spread = jnp.maximum(m2 - m1 * m1, 0.0)
    bend = jnp.maximum(m3 - 2.0 * m1 * m2 + m1 * m1 * m1, 0.0)
    beta = alpha * alpha * spread
    below = spread + bend - alpha * spread * spread
    usable = (spread > 0.0) & (below > 0.0)
    later = jnp.where(usable, jnp.minimum(spread / jnp.where(usable, below, 1.0), 1.0), 0.0)
    on_start = alpha + later * (alpha * m1 + beta)
    on_image = -later * alpha
    on_start = jnp.broadcast_to(widen(on_start, first_ref), first_ref.shape)
    on_image = jnp.broadcast_to(widen(on_image, first_ref), first_ref.shape)
    increment_ref[...] = on_start * first_ref[...] + on_image * second_ref[...]
    for m in range(start_ref.shape[0]):
        control_ref[m] = on_start * start_ref[m] + on_image * image_ref[m]


def vmem():
    return pl.BlockSpec(memory_space=pltpu.VMEM)


def elsewhere():
    return pl.BlockSpec(memory_space=pl.ANY)


def call(kernel, name, outs, args, scratch=(), specs=None, flops=0, limit=VMEM_LIMIT):
    specs = specs or {}
    moved = sum(a.size * a.dtype.itemsize for a in (*args, *outs))
    return pl.pallas_call(
        kernel,
        name=name,
        out_shape=list(outs),
        in_specs=[specs.get(i, vmem)() for i in range(len(args))],
        out_specs=[vmem()] * len(outs),
        scratch_shapes=list(scratch),
        cost_estimate=pl.CostEstimate(flops=flops, bytes_accessed=moved, transcendentals=0),
        compiler_params=pltpu.CompilerParams(vmem_limit_bytes=limit),
    )(*args)


def shape_of(*dims, dtype=F32):
    return jax.ShapeDtypeStruct(dims, dtype)


def from_partners(value, axis):
    size = lax.axis_size(axis)
    return [lax.ppermute(value, axis, [(i, i ^ step) for i in range(size)]) for step in range(1, size)]


def partner(value, axis, step):
    return lax.ppermute(value, axis, [(i, i ^ step) for i in range(lax.axis_size(axis))])


def domain_terms(value, axis):
    size = lax.axis_size(axis)
    value, step = value + partner(value, axis, 1), 2
    while 4 * step < size:
        if (size // step).bit_length() % 2:
            terms = [partner(value, axis, (k * step) ^ 1) for k in (1, 2, 3)]
            value, step = (value + terms[0]) + (terms[1] + terms[2]), 4 * step
        else:
            value, step = value + partner(value, axis, step ^ 1), 2 * step
    return [value, *(partner(value, axis, (k * step) ^ 1) for k in (1, 2, 3))]


def local(perturbations, innovations, precision_field, obs_counts, vertical_map, diffusivity):
    count, levels, size = perturbations.shape
    tiles = -(-(count + 2) // SLOTS)
    domains = lax.axis_size("domain")
    up = [(i, (i + 1) % domains) for i in range(domains)]
    down = [(j, i) for i, j in up]
    level = shape_of(levels, size)
    members_f32 = shape_of(count, levels, size)
    edge_tiles = shape_of(tiles, levels, LANES)
    moment_rows = shape_of(8, LANES)
    edge_level = shape_of(levels, LANES)
    message = shape_of(-(-tiles * HALO // SLOT), levels, LANES)
    column = shape_of(levels, levels, LANES)
    work, edge_work = count * levels * size * 50, tiles * levels * LANES * 50
    scratch = [pltpu.VMEM((count, levels, size), F32)] * 2
    edge_scratch = [pltpu.VMEM((tiles, levels, LANES), F32)] * 2

    counts = obs_counts.reshape(1, size)
    low, high, low_message, high_message = call(
        pack_kernel, "pack_edges", [edge_tiles, edge_tiles, message, message],
        (perturbations, innovations, precision_field, counts),
        [
            pltpu.VMEM((count, levels, size), perturbations.dtype), pltpu.VMEM((levels, size), F32),
            pltpu.VMEM((levels, size), F32), pltpu.VMEM((1, size), jnp.int32), pltpu.SemaphoreType.DMA((4,)),
        ],
        dict.fromkeys(range(4), elsewhere), tiles * levels * LANES * 20, None,
    )
    before = lax.ppermute(low_message, "domain", up)
    after = lax.ppermute(high_message, "domain", down)
    group = max(g for g in range(1, 6) if count % g == 0)
    blocks = shape_of(group * levels, 3 * group * levels, dtype=jnp.bfloat16)
    split = pltpu.VMEM((count // group, 3 * group * levels, size), jnp.bfloat16)
    taps, square, mapped, blocks, shifted, source, weight, main = call(
        main_kernel, "first_inner",
        [
            shape_of(3, levels, LANES), column, column, blocks, shape_of(len(SHIFTS), count, levels, size, dtype=perturbations.dtype),
            level, level, level,
        ],
        (diffusivity.reshape(1, levels), vertical_map, perturbations, innovations, precision_field, counts),
        [split, scratch[0], pltpu.VMEM((1, levels), F32), pltpu.VMEM((1, size), jnp.int32), pltpu.SemaphoreType.DMA((2,))],
        {0: elsewhere, 5: elsewhere}, work,
    )
    edge_members, edge_source, edge_weight, part = call(
        functools.partial(edge_kernel, count), "first_edges",
        [edge_tiles, edge_level, edge_level, shape_of(levels, size + LANES)],
        (low, high, before, after, taps, square, main), edge_scratch, flops=edge_work,
    )

    def adjoint(name, field, edge_field):
        (out,) = call(
            adjoint_kernel, name, [members_f32], (shifted, edge_members, field, edge_field, taps, mapped),
            [scratch[0], edge_scratch[0]], flops=work,
        )
        return out

    others = from_partners(part, "member")
    start = adjoint("start_vector", source, edge_source)
    first, weighted, edge_weighted, part = call(
        second_kernel, "second_apply", [level, level, edge_level, level],
        (shifted, edge_members, weight, edge_weight, taps, square, blocks, part, *others, start),
        [split, scratch[0], *edge_scratch], {11: elsewhere}, work + edge_work,
    )
    others = from_partners(part, "member")
    image = adjoint("image_vector", weighted, edge_weighted)
    second, moments = call(
        moments_kernel, "moments", [level, moment_rows],
        (source, weight, first, weighted, part, *others, image), (), {8: elsewhere},
    )
    moments = domain_terms(moments, "domain")
    return tuple(
        call(final_kernel, "combine", [members_f32, level], (*moments, start, image, first, second))
    )


def solution(mesh):
    in_specs = (
        P("member", None, "domain"),
        P(None, "domain"),
        P(None, "domain"),
        P("domain"),
        P(),
        P(),
    )
    out_specs = (P("member", None, "domain"), P(None, "domain"))
    return jax.shard_map(local, mesh=mesh, in_specs=in_specs, out_specs=out_specs, check_vma=False)
```

```python
import functools

import jax
import jax.numpy as jnp
from jax import lax
from jax.experimental import pallas as pl
from jax.experimental.pallas import tpu as pltpu
from jax.sharding import PartitionSpec as P

DIFF = 2
LANES = 128
REACH = 2 * DIFF
HALO = 2 * REACH
SLOT = 4 * HALO
SLOTS = LANES // SLOT
SHIFTS = range(-DIFF, DIFF + 1)
F32 = jnp.float32
HIGHEST = lax.Precision.HIGHEST
VMEM_LIMIT = 32 * 1024 * 1024


def lane_roll(value, shift):
    return pltpu.roll(value, shift % value.shape[-1], value.ndim - 1)


def lane_index(shape):
    return lax.broadcasted_iota(jnp.int32, shape, len(shape) - 1)


def widen(column, like):
    copies = like.shape[-1] // LANES
    return column if copies == 1 else jnp.concatenate([column] * copies, axis=-1)


def level_column(row):
    levels = row.shape[1]
    square = jnp.broadcast_to(row, (levels, levels))
    own = lax.broadcasted_iota(jnp.int32, square.shape, 0) == lane_index(square.shape)
    return jnp.broadcast_to(jnp.sum(jnp.where(own, square, 0.0), axis=1, keepdims=True), (levels, LANES))


def smooth(field, taps):
    near = lane_roll(field, 1) + lane_roll(field, -1)
    far = lane_roll(field, 2) + lane_roll(field, -2)
    return taps[0] * field + taps[1] * near + taps[2] * far


def mixed(mix_ref, field_ref):
    out = None
    for k in range(mix_ref.shape[0]):
        row = field_ref[k : k + 1, :]
        term = widen(mix_ref[k], row) * row
        out = term if out is None else out + term
    return out


def wide_taps(taps_ref, like):
    return [widen(taps_ref[i], like) for i in range(3)]


def shifted_by(value, shift):
    return value if shift == 0 else lane_roll(value, shift)


def smooth_product(shifted_ref, m, steps):
    out = None
    for i, step in enumerate(steps):
        term = shifted_ref[i, m].astype(F32) * step
        out = term if out is None else out + term
    return out


def field_steps(field, taps_ref):
    taps = wide_taps(taps_ref, field)
    return [taps[abs(s)] * shifted_by(field, s) for s in SHIFTS]


def apply_shifted(shifted_ref, field, taps_ref, blocks_ref, split_ref, y_ref):
    _, count, levels, size = shifted_ref.shape
    rows = blocks_ref.shape[0]
    group = rows // levels
    steps = field_steps(field, taps_ref)
    for m in range(count):
        value = smooth_product(shifted_ref, m, steps)
        high = value.astype(jnp.bfloat16)
        low = (value - high.astype(F32)).astype(jnp.bfloat16)
        place, at = m // group, m % group * levels
        for base, part in ((0, high), (rows, high), (2 * rows, low)):
            split_ref[place, base + at : base + at + levels] = part
    for place in range(count // group):
        value = jnp.dot(blocks_ref[...], split_ref[place], preferred_element_type=F32)
        y_ref[place * group : (place + 1) * group] = value.reshape(group, levels, size)
    totals = [jnp.zeros((levels, size), F32)] * len(SHIFTS)
    for m in range(count):
        value = y_ref[m]
        totals = [total + shifted_ref[i, m].astype(F32) * value for i, total in enumerate(totals)]
    taps = wide_taps(taps_ref, field)
    return sum(taps[abs(s)] * shifted_by(total, -s) for s, total in zip(SHIFTS, totals))


def apply_ensemble(parts, taps_ref, mix_ref, scratches):
    totals = []
    for (members_ref, field), (x_ref, y_ref) in zip(parts, scratches):
        taps = wide_taps(taps_ref, field)
        for m in range(members_ref.shape[0]):
            x_ref[m] = smooth(members_ref[m].astype(F32) * field, taps)
    for (members_ref, field), (x_ref, y_ref) in zip(parts, scratches):
        for m in range(members_ref.shape[0]):
            y_ref[m] = mixed(mix_ref, x_ref.at[m])
    for (members_ref, field), (x_ref, y_ref) in zip(parts, scratches):
        taps = wide_taps(taps_ref, field)
        total = jnp.zeros(field.shape, F32)
        for m in range(members_ref.shape[0]):
            total = total + members_ref[m].astype(F32) * smooth(y_ref[m], taps)
        totals.append(total)
    return totals


def all_slots(value):
    one, two, three = (lane_roll(value, k * SLOT) for k in (1, 2, 3))
    return (value + two) + (one + three)


def ends_of(first, last, lane):
    return jnp.where(lane < HALO, first, jnp.where(lane >= LANES - HALO, last, 0.0))


def added(total, term):
    return term if total is None else total + term


def patch(main, edge, width, slot=0):
    size = main.shape[-1]
    first = lane_roll(edge, -(slot * SLOT + HALO))
    last = lane_roll(edge, -(slot * SLOT + 3 * HALO))
    lane = lane_index(main.shape)
    out = jnp.where(lane < width, widen(first, main), main)
    return jnp.where(lane >= size - width, widen(last, main), out)


def pack_kernel(
    members_hbm, innovations_hbm, precision_hbm, counts_hbm,
    low_ref, high_ref, low_message_ref, high_message_ref,
    members_ref, innovations_ref, precision_ref, counts_ref, sems,
):
    copies = [
        pltpu.make_async_copy(source, target, sems.at[i])
        for i, (source, target) in enumerate(
            (
                (members_hbm, members_ref),
                (innovations_hbm, innovations_ref),
                (precision_hbm, precision_ref),
                (counts_hbm, counts_ref),
            )
        )
    ]
    for copy in copies:
        copy.start()
    for copy in copies[1:]:
        copy.wait()
    weight = counts_ref[...].astype(F32) * precision_ref[...]
    fields = (weight * innovations_ref[...], weight)
    copies[0].wait()
    count, levels, size = members_ref.shape
    lane = lane_index((levels, LANES))
    at = lane % SLOT
    low_message, high_message = [None] * low_message_ref.shape[0], [None] * low_message_ref.shape[0]
    for tile in range(low_ref.shape[0]):
        low = high = None
        for slot in range(SLOTS):
            m = tile * SLOTS + slot
            if m < count:
                first, last = members_ref[m, :, :LANES].astype(F32), members_ref[m, :, size - LANES :].astype(F32)
            elif m < count + 2:
                first, last = fields[m - count][:, :LANES], fields[m - count][:, size - LANES :]
            else:
                continue
            ends = ends_of(first, last, lane)
            low = added(low, lane_roll(ends, slot * SLOT + HALO))
            high = added(high, lane_roll(ends, slot * SLOT + 3 * HALO))
        low_ref[tile] = low
        high_ref[tile] = high
        place, shift = divmod(tile, SLOT // HALO)
        low_message[place] = added(low_message[place], lane_roll(jnp.where(at < HALO, low, 0.0), shift * HALO))
        high = lane_roll(jnp.where(at >= 3 * HALO, high, 0.0), shift * HALO - 3 * HALO)
        high_message[place] = added(high_message[place], high)
    for place in range(low_message_ref.shape[0]):
        low_message_ref[place] = low_message[place]
        high_message_ref[place] = high_message[place]


def main_kernel(
    diffusivity_ref, map_ref, members_ref, innovations_ref, precision_ref, counts_ref,
    taps_ref, square_ref, adjoint_ref, blocks_ref, shifted_ref, source_ref, weight_ref, out_ref,
    split_ref, y_ref,
):
    levels = members_ref.shape[1]
    matrix = map_ref[...]
    dims = (((1,), (1,)), ((), ()))
    square = lax.dot_general(matrix, matrix, dims, precision=HIGHEST, preferred_element_type=F32)
    turned = matrix.T
    rows, width = blocks_ref.shape
    column = lane_index((levels, -(-width // LANES) * LANES))
    block = jnp.zeros(column.shape, F32)
    for k in range(levels):
        square_ref[k] = jnp.broadcast_to(square[:, k : k + 1], (levels, LANES))
        block = jnp.where(column % levels == k, widen(square_ref[k], block), block)
        adjoint_ref[k] = jnp.broadcast_to(turned[:, k : k + 1], (levels, LANES))
    high = block.astype(jnp.bfloat16).astype(F32)
    block = jnp.where(column // rows == 1, block - high, high)
    for i in range(rows // levels):
        value = jnp.where(column % rows // levels == i, block, 0.0).astype(jnp.bfloat16)
        blocks_ref[i * levels : (i + 1) * levels] = value[:, :width]
    for m in range(members_ref.shape[0]):
        value = members_ref[m].astype(F32)
        for i, s in enumerate(SHIFTS):
            shifted_ref[i, m] = shifted_by(value, s).astype(shifted_ref.dtype)
    coef = level_column(diffusivity_ref[...])
    keep = 1.0 - 2.0 * coef
    taps_ref[0] = keep * keep + 2.0 * coef * coef
    taps_ref[1] = 2.0 * keep * coef
    taps_ref[2] = coef * coef
    weight = counts_ref[...].astype(F32) * precision_ref[...]
    source = weight * innovations_ref[...]
    source_ref[...], weight_ref[...] = source, weight
    out_ref[...] = apply_shifted(shifted_ref, source, taps_ref, blocks_ref, split_ref, y_ref)


def edge_kernel(
    count, low_ref, high_ref, before_ref, after_ref, taps_ref, square_ref, main_ref,
    edge_members_ref, edge_source_ref, edge_weight_ref, out_ref, x_ref, y_ref,
):
    tiles, levels, _ = low_ref.shape
    size = main_ref.shape[1]
    lane = lane_index((levels, LANES))
    at, slot_of = lane % SLOT, lane // SLOT
    for tile in range(tiles):
        place, shift = divmod(tile, SLOT // HALO)
        before = lane_roll(before_ref[place], -shift * HALO)
        after = lane_roll(after_ref[place], (3 - shift) * HALO)
        own = jnp.where(at >= 2 * HALO, high_ref[tile], low_ref[tile])
        value = jnp.where(at >= 3 * HALO, after, jnp.where(at < HALO, before, own))
        for i, field_ref in enumerate((edge_source_ref, edge_weight_ref)):
            place, slot = divmod(count + i, SLOTS)
            if place == tile:
                field_ref[...] = all_slots(jnp.where(slot_of == slot, value, 0.0))
        held = min(max(count - tile * SLOTS, 0), SLOTS)
        edge_members_ref[tile] = value if held == SLOTS else jnp.where(slot_of < held, value, 0.0)
    (edge,) = apply_ensemble([(edge_members_ref, edge_source_ref[...])], taps_ref, square_ref, [(x_ref, y_ref)])
    edge = all_slots(edge)
    out_ref[:, :size] = patch(main_ref[...], edge, REACH)
    out_ref[:, size:] = edge


def tree_sum(own_ref, a_ref, b_ref, c_ref):
    return (own_ref[...] + a_ref[...]) + (b_ref[...] + c_ref[...])


def second_kernel(
    shifted_ref, edge_members_ref, weight_ref, edge_weight_ref, taps_ref, square_ref, blocks_ref,
    own_ref, a_ref, b_ref, c_ref, _,
    first_ref, weighted_ref, edge_weighted_ref, out_ref, split_ref, y_ref, edge_x_ref, edge_y_ref,
):
    levels, size = weight_ref.shape
    lane = lane_index((levels, LANES))
    at = lane % SLOT
    total = tree_sum(own_ref, a_ref, b_ref, c_ref)
    first, edge = total[:, :size], total[:, size:]
    ends = ends_of(first[:, :LANES], first[:, size - LANES :], lane)
    own = jnp.where(lane >= 2 * HALO, lane_roll(ends, 3 * HALO), lane_roll(ends, HALO))
    own = all_slots(jnp.where(lane < SLOT, own, 0.0))
    edge = jnp.where((at >= HALO) & (at < 3 * HALO), own, edge)
    weighted = weight_ref[...] * first
    edge_weighted = edge_weight_ref[...] * edge
    first_ref[...] = first
    weighted_ref[...] = weighted
    edge_weighted_ref[...] = edge_weighted
    main = apply_shifted(shifted_ref, weighted, taps_ref, blocks_ref, split_ref, y_ref)
    (edge,) = apply_ensemble(
        [(edge_members_ref, edge_weighted)], taps_ref, square_ref, [(edge_x_ref, edge_y_ref)]
    )
    out_ref[...] = patch(main, all_slots(edge), REACH)


def moments_kernel(
    source_ref, weight_ref, first_ref, weighted_ref, own_ref, a_ref, b_ref, c_ref, _, second_ref, moments_ref
):
    size = first_ref.shape[1]
    source, weight = source_ref[...], weight_ref[...]
    first, weighted = first_ref[...], weighted_ref[...]
    second = tree_sum(own_ref, a_ref, b_ref, c_ref)
    second_ref[...] = second
    kind = lax.broadcasted_iota(jnp.int32, moments_ref.shape, 0)
    out = jnp.zeros(moments_ref.shape, F32)
    for i, product in enumerate((source * first, weighted * first, weighted * second, weight * second * second)):
        row = sum(product[:, at : at + LANES] for at in range(0, size, LANES))
        out = jnp.where(kind == i, jnp.sum(row, axis=0, keepdims=True), out)
    moments_ref[...] = out


def adjoint_kernel(
    shifted_ref, edge_members_ref, field_ref, edge_field_ref, taps_ref, adjoint_ref, out_ref, x_ref, edge_x_ref
):
    field, edge_field = field_ref[...], edge_field_ref[...]
    steps, edge_taps = field_steps(field, taps_ref), wide_taps(taps_ref, edge_field)
    for tile in range(edge_members_ref.shape[0]):
        edge_x_ref[tile] = smooth(edge_members_ref[tile] * edge_field, edge_taps)
    for m in range(out_ref.shape[0]):
        main = smooth_product(shifted_ref, m, steps)
        x_ref[m] = patch(main, edge_x_ref[m // SLOTS], DIFF, m % SLOTS)
    for m in range(out_ref.shape[0]):
        out_ref[m] = mixed(adjoint_ref, x_ref.at[m])


def final_kernel(
    own_ref, a_ref, b_ref, c_ref, start_ref, image_ref, first_ref, second_ref, control_ref, increment_ref
):
    total = tree_sum(own_ref, a_ref, b_ref, c_ref)
    total = jnp.broadcast_to(jnp.sum(total, axis=1, keepdims=True), total.shape)
    mu = [total[i : i + 1, :] for i in range(4)]
    alpha = mu[0] / (mu[0] + mu[1])
    scale = 1.0 / mu[0]
    m1, m2, m3 = (value * scale for value in mu[1:])
    spread = jnp.maximum(m2 - m1 * m1, 0.0)
    bend = jnp.maximum(m3 - 2.0 * m1 * m2 + m1 * m1 * m1, 0.0)
    beta = alpha * alpha * spread
    below = spread + bend - alpha * spread * spread
    usable = (spread > 0.0) & (below > 0.0)
    later = jnp.where(usable, jnp.minimum(spread / jnp.where(usable, below, 1.0), 1.0), 0.0)
    on_start = alpha + later * (alpha * m1 + beta)
    on_image = -later * alpha
    on_start = jnp.broadcast_to(widen(on_start, first_ref), first_ref.shape)
    on_image = jnp.broadcast_to(widen(on_image, first_ref), first_ref.shape)
    increment_ref[...] = on_start * first_ref[...] + on_image * second_ref[...]
    for m in range(start_ref.shape[0]):
        control_ref[m] = on_start * start_ref[m] + on_image * image_ref[m]


def vmem():
    return pl.BlockSpec(memory_space=pltpu.VMEM)


def elsewhere():
    return pl.BlockSpec(memory_space=pl.ANY)


def call(kernel, name, outs, args, scratch=(), specs=None, flops=0, limit=VMEM_LIMIT):
    specs = specs or {}
    moved = sum(a.size * a.dtype.itemsize for a in (*args, *outs))
    return pl.pallas_call(
        kernel,
        name=name,
        out_shape=list(outs),
        in_specs=[specs.get(i, vmem)() for i in range(len(args))],
        out_specs=[vmem()] * len(outs),
        scratch_shapes=list(scratch),
        cost_estimate=pl.CostEstimate(flops=flops, bytes_accessed=moved, transcendentals=0),
        compiler_params=pltpu.CompilerParams(vmem_limit_bytes=limit),
    )(*args)


def shape_of(*dims, dtype=F32):
    return jax.ShapeDtypeStruct(dims, dtype)


def from_partners(value, axis):
    size = lax.axis_size(axis)
    return [lax.ppermute(value, axis, [(i, i ^ step) for i in range(size)]) for step in range(1, size)]


def partner(value, axis, step):
    return lax.ppermute(value, axis, [(i, i ^ step) for i in range(lax.axis_size(axis))])


def domain_terms(value, axis):
    size = lax.axis_size(axis)
    value, step = value + partner(value, axis, 1), 2
    while 4 * step < size:
        if (size // step).bit_length() % 2:
            terms = [partner(value, axis, (k * step) ^ 1) for k in (1, 2, 3)]
            value, step = (value + terms[0]) + (terms[1] + terms[2]), 4 * step
        else:
            value, step = value + partner(value, axis, step ^ 1), 2 * step
    return [value, *(partner(value, axis, (k * step) ^ 1) for k in (1, 2, 3))]


def local(perturbations, innovations, precision_field, obs_counts, vertical_map, diffusivity):
    count, levels, size = perturbations.shape
    tiles = -(-(count + 2) // SLOTS)
    domains = lax.axis_size("domain")
    up = [(i, (i + 1) % domains) for i in range(domains)]
    down = [(j, i) for i, j in up]
    level = shape_of(levels, size)
    members_f32 = shape_of(count, levels, size)
    edge_tiles = shape_of(tiles, levels, LANES)
    moment_rows = shape_of(8, LANES)
    edge_level = shape_of(levels, LANES)
    message = shape_of(-(-tiles * HALO // SLOT), levels, LANES)
    column = shape_of(levels, levels, LANES)
    work, edge_work = count * levels * size * 50, tiles * levels * LANES * 50
    scratch = [pltpu.VMEM((count, levels, size), F32)] * 2
    edge_scratch = [pltpu.VMEM((tiles, levels, LANES), F32)] * 2

    counts = obs_counts.reshape(1, size)
    low, high, low_message, high_message = call(
        pack_kernel, "pack_edges", [edge_tiles, edge_tiles, message, message],
        (perturbations, innovations, precision_field, counts),
        [
            pltpu.VMEM((count, levels, size), perturbations.dtype), pltpu.VMEM((levels, size), F32),
            pltpu.VMEM((levels, size), F32), pltpu.VMEM((1, size), jnp.int32), pltpu.SemaphoreType.DMA((4,)),
        ],
        dict.fromkeys(range(4), elsewhere), tiles * levels * LANES * 20, None,
    )
    before = lax.ppermute(low_message, "domain", up)
    after = lax.ppermute(high_message, "domain", down)
    group = max(g for g in range(1, 6) if count % g == 0)
    blocks = shape_of(group * levels, 3 * group * levels, dtype=jnp.bfloat16)
    split = pltpu.VMEM((count // group, 3 * group * levels, size), jnp.bfloat16)
    taps, square, mapped, blocks, shifted, source, weight, main = call(
        main_kernel, "first_inner",
        [
            shape_of(3, levels, LANES), column, column, blocks, shape_of(len(SHIFTS), count, levels, size, dtype=perturbations.dtype),
            level, level, level,
        ],
        (diffusivity.reshape(1, levels), vertical_map, perturbations, innovations, precision_field, counts),
        [split, scratch[0]], flops=work,
    )
    edge_members, edge_source, edge_weight, part = call(
        functools.partial(edge_kernel, count), "first_edges",
        [edge_tiles, edge_level, edge_level, shape_of(levels, size + LANES)],
        (low, high, before, after, taps, square, main), edge_scratch, flops=edge_work,
    )

    def adjoint(name, field, edge_field):
        (out,) = call(
            adjoint_kernel, name, [members_f32], (shifted, edge_members, field, edge_field, taps, mapped),
            [scratch[0], edge_scratch[0]], flops=work,
        )
        return out

    others = from_partners(part, "member")
    start = adjoint("start_vector", source, edge_source)
    first, weighted, edge_weighted, part = call(
        second_kernel, "second_apply", [level, level, edge_level, level],
        (shifted, edge_members, weight, edge_weight, taps, square, blocks, part, *others, start),
        [split, scratch[0], *edge_scratch], {11: elsewhere}, work + edge_work,
    )
    others = from_partners(part, "member")
    image = adjoint("image_vector", weighted, edge_weighted)
    second, moments = call(
        moments_kernel, "moments", [level, moment_rows],
        (source, weight, first, weighted, part, *others, image), (), {8: elsewhere},
    )
    moments = domain_terms(moments, "domain")
    return tuple(
        call(final_kernel, "combine", [members_f32, level], (*moments, start, image, first, second))
    )


def solution(mesh):
    in_specs = (
        P("member", None, "domain"),
        P(None, "domain"),
        P(None, "domain"),
        P("domain"),
        P(),
        P(),
    )
    out_specs = (P("member", None, "domain"), P(None, "domain"))
    return jax.shard_map(local, mesh=mesh, in_specs=in_specs, out_specs=out_specs, check_vma=False)
```

```python
import functools

import jax
import jax.numpy as jnp
from jax import lax
from jax.experimental import pallas as pl
from jax.experimental.pallas import tpu as pltpu
from jax.sharding import PartitionSpec as P

DIFF = 2
LANES = 128
REACH = 2 * DIFF
HALO = 2 * REACH
SLOT = 4 * HALO
SLOTS = LANES // SLOT
SHIFTS = range(-DIFF, DIFF + 1)
F32 = jnp.float32
HIGHEST = lax.Precision.HIGHEST
VMEM_LIMIT = 32 * 1024 * 1024


def lane_roll(value, shift):
    return pltpu.roll(value, shift % value.shape[-1], value.ndim - 1)


def lane_index(shape):
    return lax.broadcasted_iota(jnp.int32, shape, len(shape) - 1)


def widen(column, like):
    copies = like.shape[-1] // LANES
    return column if copies == 1 else jnp.concatenate([column] * copies, axis=-1)


def level_column(row):
    levels = row.shape[1]
    square = jnp.broadcast_to(row, (levels, levels))
    own = lax.broadcasted_iota(jnp.int32, square.shape, 0) == lane_index(square.shape)
    return jnp.broadcast_to(jnp.sum(jnp.where(own, square, 0.0), axis=1, keepdims=True), (levels, LANES))


def smooth(field, taps):
    near = lane_roll(field, 1) + lane_roll(field, -1)
    far = lane_roll(field, 2) + lane_roll(field, -2)
    return taps[0] * field + taps[1] * near + taps[2] * far


def mixed(mix_ref, field_ref):
    out = None
    for k in range(mix_ref.shape[0]):
        row = field_ref[k : k + 1, :]
        term = widen(mix_ref[k], row) * row
        out = term if out is None else out + term
    return out


def wide_taps(taps_ref, like):
    return [widen(taps_ref[i], like) for i in range(3)]


def shifted_by(value, shift):
    return value if shift == 0 else lane_roll(value, shift)


def smooth_product(shifted_ref, m, steps):
    out = None
    for i, step in enumerate(steps):
        term = shifted_ref[i, m].astype(F32) * step
        out = term if out is None else out + term
    return out


def field_steps(field, taps_ref):
    taps = wide_taps(taps_ref, field)
    return [taps[abs(s)] * shifted_by(field, s) for s in SHIFTS]


def apply_shifted(shifted_ref, field, taps_ref, blocks_ref, split_ref, y_ref):
    _, count, levels, size = shifted_ref.shape
    rows = blocks_ref.shape[0]
    group = rows // levels
    steps = field_steps(field, taps_ref)
    for m in range(count):
        value = smooth_product(shifted_ref, m, steps)
        high = value.astype(jnp.bfloat16)
        low = (value - high.astype(F32)).astype(jnp.bfloat16)
        place, at = m // group, m % group * levels
        for base, part in ((0, high), (rows, high), (2 * rows, low)):
            split_ref[place, base + at : base + at + levels] = part
    for place in range(count // group):
        value = jnp.dot(blocks_ref[...], split_ref[place], preferred_element_type=F32)
        y_ref[place * group : (place + 1) * group] = value.reshape(group, levels, size)
    totals = [jnp.zeros((levels, size), F32)] * len(SHIFTS)
    for m in range(count):
        value = y_ref[m]
        totals = [total + shifted_ref[i, m].astype(F32) * value for i, total in enumerate(totals)]
    taps = wide_taps(taps_ref, field)
    return sum(taps[abs(s)] * shifted_by(total, -s) for s, total in zip(SHIFTS, totals))


def apply_ensemble(parts, taps_ref, mix_ref, scratches):
    totals = []
    for (members_ref, field), (x_ref, y_ref) in zip(parts, scratches):
        taps = wide_taps(taps_ref, field)
        for m in range(members_ref.shape[0]):
            x_ref[m] = smooth(members_ref[m].astype(F32) * field, taps)
    for (members_ref, field), (x_ref, y_ref) in zip(parts, scratches):
        for m in range(members_ref.shape[0]):
            y_ref[m] = mixed(mix_ref, x_ref.at[m])
    for (members_ref, field), (x_ref, y_ref) in zip(parts, scratches):
        taps = wide_taps(taps_ref, field)
        total = jnp.zeros(field.shape, F32)
        for m in range(members_ref.shape[0]):
            total = total + members_ref[m].astype(F32) * smooth(y_ref[m], taps)
        totals.append(total)
    return totals


def all_slots(value):
    one, two, three = (lane_roll(value, k * SLOT) for k in (1, 2, 3))
    return (value + two) + (one + three)


def ends_of(first, last, lane):
    return jnp.where(lane < HALO, first, jnp.where(lane >= LANES - HALO, last, 0.0))


def added(total, term):
    return term if total is None else total + term


def patch(main, edge, width, slot=0):
    size = main.shape[-1]
    first = lane_roll(edge, -(slot * SLOT + HALO))
    last = lane_roll(edge, -(slot * SLOT + 3 * HALO))
    lane = lane_index(main.shape)
    out = jnp.where(lane < width, widen(first, main), main)
    return jnp.where(lane >= size - width, widen(last, main), out)


def pack_kernel(
    members_hbm, innovations_hbm, precision_hbm, counts_hbm,
    low_ref, high_ref, low_message_ref, high_message_ref,
    members_ref, innovations_ref, precision_ref, counts_ref, sems,
):
    copies = [
        pltpu.make_async_copy(source, target, sems.at[i])
        for i, (source, target) in enumerate(
            (
                (members_hbm, members_ref),
                (innovations_hbm, innovations_ref),
                (precision_hbm, precision_ref),
                (counts_hbm, counts_ref),
            )
        )
    ]
    for copy in copies:
        copy.start()
    for copy in copies[1:]:
        copy.wait()
    weight = counts_ref[...].astype(F32) * precision_ref[...]
    fields = (weight * innovations_ref[...], weight)
    copies[0].wait()
    count, levels, size = members_ref.shape
    lane = lane_index((levels, LANES))
    at = lane % SLOT
    low_message, high_message = [None] * low_message_ref.shape[0], [None] * low_message_ref.shape[0]
    for tile in range(low_ref.shape[0]):
        low = None
        for slot in range(SLOTS):
            m = tile * SLOTS + slot
            if m < count:
                first, last = members_ref[m, :, :LANES].astype(F32), members_ref[m, :, size - LANES :].astype(F32)
            elif m < count + 2:
                first, last = fields[m - count][:, :LANES], fields[m - count][:, size - LANES :]
            else:
                continue
            ends = ends_of(first, last, lane)
            low = added(low, lane_roll(ends, slot * SLOT + HALO))
        low_ref[tile] = low
        high_ref[tile] = lane_roll(low, 2 * HALO)
        place, shift = divmod(tile, SLOT // HALO)
        low_message[place] = added(low_message[place], lane_roll(jnp.where(at < HALO, low, 0.0), shift * HALO))
        first = jnp.where((at >= HALO) & (at < 2 * HALO), low, 0.0)
        high_message[place] = added(high_message[place], lane_roll(first, shift * HALO - HALO))
    for place in range(low_message_ref.shape[0]):
        low_message_ref[place] = low_message[place]
        high_message_ref[place] = high_message[place]


def main_kernel(
    diffusivity_ref, map_ref, members_ref, innovations_ref, precision_ref, counts_ref,
    taps_ref, square_ref, adjoint_ref, blocks_ref, shifted_ref, source_ref, weight_ref, out_ref,
    split_ref, y_ref,
):
    levels = members_ref.shape[1]
    matrix = map_ref[...]
    dims = (((1,), (1,)), ((), ()))
    square = lax.dot_general(matrix, matrix, dims, precision=HIGHEST, preferred_element_type=F32)
    turned = matrix.T
    rows, width = blocks_ref.shape
    column = lane_index((levels, -(-width // LANES) * LANES))
    block = jnp.zeros(column.shape, F32)
    for k in range(levels):
        square_ref[k] = jnp.broadcast_to(square[:, k : k + 1], (levels, LANES))
        block = jnp.where(column % levels == k, widen(square_ref[k], block), block)
        adjoint_ref[k] = jnp.broadcast_to(turned[:, k : k + 1], (levels, LANES))
    high = block.astype(jnp.bfloat16).astype(F32)
    block = jnp.where(column // rows == 1, block - high, high)
    for i in range(rows // levels):
        value = jnp.where(column % rows // levels == i, block, 0.0).astype(jnp.bfloat16)
        blocks_ref[i * levels : (i + 1) * levels] = value[:, :width]
    for m in range(members_ref.shape[0]):
        value = members_ref[m].astype(F32)
        for i, s in enumerate(SHIFTS):
            shifted_ref[i, m] = shifted_by(value, s).astype(shifted_ref.dtype)
    coef = level_column(diffusivity_ref[...])
    keep = 1.0 - 2.0 * coef
    taps_ref[0] = keep * keep + 2.0 * coef * coef
    taps_ref[1] = 2.0 * keep * coef
    taps_ref[2] = coef * coef
    weight = counts_ref[...].astype(F32) * precision_ref[...]
    source = weight * innovations_ref[...]
    source_ref[...], weight_ref[...] = source, weight
    out_ref[...] = apply_shifted(shifted_ref, source, taps_ref, blocks_ref, split_ref, y_ref)


def edge_kernel(
    count, low_ref, high_ref, before_ref, after_ref, taps_ref, square_ref, main_ref,
    edge_members_ref, edge_source_ref, edge_weight_ref, out_ref, x_ref, y_ref,
):
    tiles, levels, _ = low_ref.shape
    size = main_ref.shape[1]
    lane = lane_index((levels, LANES))
    at, slot_of = lane % SLOT, lane // SLOT
    for tile in range(tiles):
        place, shift = divmod(tile, SLOT // HALO)
        before = lane_roll(before_ref[place], -shift * HALO)
        after = lane_roll(after_ref[place], (3 - shift) * HALO)
        own = jnp.where(at >= 2 * HALO, high_ref[tile], low_ref[tile])
        value = jnp.where(at >= 3 * HALO, after, jnp.where(at < HALO, before, own))
        for i, field_ref in enumerate((edge_source_ref, edge_weight_ref)):
            place, slot = divmod(count + i, SLOTS)
            if place == tile:
                field_ref[...] = all_slots(jnp.where(slot_of == slot, value, 0.0))
        held = min(max(count - tile * SLOTS, 0), SLOTS)
        edge_members_ref[tile] = value if held == SLOTS else jnp.where(slot_of < held, value, 0.0)
    (edge,) = apply_ensemble([(edge_members_ref, edge_source_ref[...])], taps_ref, square_ref, [(x_ref, y_ref)])
    edge = all_slots(edge)
    out_ref[:, :size] = patch(main_ref[...], edge, REACH)
    out_ref[:, size:] = edge


def tree_sum(own_ref, a_ref, b_ref, c_ref):
    return (own_ref[...] + a_ref[...]) + (b_ref[...] + c_ref[...])


def second_kernel(
    shifted_ref, edge_members_ref, weight_ref, edge_weight_ref, taps_ref, square_ref, blocks_ref,
    own_ref, a_ref, b_ref, c_ref, _,
    first_ref, weighted_ref, edge_weighted_ref, out_ref, split_ref, y_ref, edge_x_ref, edge_y_ref,
):
    levels, size = weight_ref.shape
    lane = lane_index((levels, LANES))
    at = lane % SLOT
    total = tree_sum(own_ref, a_ref, b_ref, c_ref)
    first, edge = total[:, :size], total[:, size:]
    ends = ends_of(first[:, :LANES], first[:, size - LANES :], lane)
    own = jnp.where(lane >= 2 * HALO, lane_roll(ends, 3 * HALO), lane_roll(ends, HALO))
    own = all_slots(jnp.where(lane < SLOT, own, 0.0))
    edge = jnp.where((at >= HALO) & (at < 3 * HALO), own, edge)
    weighted = weight_ref[...] * first
    edge_weighted = edge_weight_ref[...] * edge
    first_ref[...] = first
    weighted_ref[...] = weighted
    edge_weighted_ref[...] = edge_weighted
    main = apply_shifted(shifted_ref, weighted, taps_ref, blocks_ref, split_ref, y_ref)
    (edge,) = apply_ensemble(
        [(edge_members_ref, edge_weighted)], taps_ref, square_ref, [(edge_x_ref, edge_y_ref)]
    )
    out_ref[...] = patch(main, all_slots(edge), REACH)


def moments_kernel(
    source_ref, weight_ref, first_ref, weighted_ref, own_ref, a_ref, b_ref, c_ref, _, second_ref, moments_ref
):
    size = first_ref.shape[1]
    source, weight = source_ref[...], weight_ref[...]
    first, weighted = first_ref[...], weighted_ref[...]
    second = tree_sum(own_ref, a_ref, b_ref, c_ref)
    second_ref[...] = second
    kind = lax.broadcasted_iota(jnp.int32, moments_ref.shape, 0)
    out = jnp.zeros(moments_ref.shape, F32)
    for i, product in enumerate((source * first, weighted * first, weighted * second, weight * second * second)):
        row = sum(product[:, at : at + LANES] for at in range(0, size, LANES))
        out = jnp.where(kind == i, jnp.sum(row, axis=0, keepdims=True), out)
    moments_ref[...] = out


def adjoint_kernel(
    shifted_ref, edge_members_ref, field_ref, edge_field_ref, taps_ref, adjoint_ref, out_ref, x_ref, edge_x_ref
):
    field, edge_field = field_ref[...], edge_field_ref[...]
    steps, edge_taps = field_steps(field, taps_ref), wide_taps(taps_ref, edge_field)
    for tile in range(edge_members_ref.shape[0]):
        edge_x_ref[tile] = smooth(edge_members_ref[tile] * edge_field, edge_taps)
    for m in range(out_ref.shape[0]):
        main = smooth_product(shifted_ref, m, steps)
        x_ref[m] = patch(main, edge_x_ref[m // SLOTS], DIFF, m % SLOTS)
    for m in range(out_ref.shape[0]):
        out_ref[m] = mixed(adjoint_ref, x_ref.at[m])


def final_kernel(
    own_ref, a_ref, b_ref, c_ref, start_ref, image_ref, first_ref, second_ref, control_ref, increment_ref
):
    total = tree_sum(own_ref, a_ref, b_ref, c_ref)
    total = jnp.broadcast_to(jnp.sum(total, axis=1, keepdims=True), total.shape)
    mu = [total[i : i + 1, :] for i in range(4)]
    alpha = mu[0] / (mu[0] + mu[1])
    scale = 1.0 / mu[0]
    m1, m2, m3 = (value * scale for value in mu[1:])
    spread = jnp.maximum(m2 - m1 * m1, 0.0)
    bend = jnp.maximum(m3 - 2.0 * m1 * m2 + m1 * m1 * m1, 0.0)
    beta = alpha * alpha * spread
    below = spread + bend - alpha * spread * spread
    usable = (spread > 0.0) & (below > 0.0)
    later = jnp.where(usable, jnp.minimum(spread / jnp.where(usable, below, 1.0), 1.0), 0.0)
    on_start = alpha + later * (alpha * m1 + beta)
    on_image = -later * alpha
    on_start = jnp.broadcast_to(widen(on_start, first_ref), first_ref.shape)
    on_image = jnp.broadcast_to(widen(on_image, first_ref), first_ref.shape)
    increment_ref[...] = on_start * first_ref[...] + on_image * second_ref[...]
    for m in range(start_ref.shape[0]):
        control_ref[m] = on_start * start_ref[m] + on_image * image_ref[m]


def vmem():
    return pl.BlockSpec(memory_space=pltpu.VMEM)


def elsewhere():
    return pl.BlockSpec(memory_space=pl.ANY)


def call(kernel, name, outs, args, scratch=(), specs=None, flops=0, limit=VMEM_LIMIT):
    specs = specs or {}
    moved = sum(a.size * a.dtype.itemsize for a in (*args, *outs))
    return pl.pallas_call(
        kernel,
        name=name,
        out_shape=list(outs),
        in_specs=[specs.get(i, vmem)() for i in range(len(args))],
        out_specs=[vmem()] * len(outs),
        scratch_shapes=list(scratch),
        cost_estimate=pl.CostEstimate(flops=flops, bytes_accessed=moved, transcendentals=0),
        compiler_params=pltpu.CompilerParams(vmem_limit_bytes=limit),
    )(*args)


def shape_of(*dims, dtype=F32):
    return jax.ShapeDtypeStruct(dims, dtype)


def from_partners(value, axis):
    size = lax.axis_size(axis)
    return [lax.ppermute(value, axis, [(i, i ^ step) for i in range(size)]) for step in range(1, size)]


def partner(value, axis, step):
    return lax.ppermute(value, axis, [(i, i ^ step) for i in range(lax.axis_size(axis))])


def domain_terms(value, axis):
    size = lax.axis_size(axis)
    value, step = value + partner(value, axis, 1), 2
    while 4 * step < size:
        if (size // step).bit_length() % 2:
            terms = [partner(value, axis, (k * step) ^ 1) for k in (1, 2, 3)]
            value, step = (value + terms[0]) + (terms[1] + terms[2]), 4 * step
        else:
            value, step = value + partner(value, axis, step ^ 1), 2 * step
    return [value, *(partner(value, axis, (k * step) ^ 1) for k in (1, 2, 3))]


def local(perturbations, innovations, precision_field, obs_counts, vertical_map, diffusivity):
    count, levels, size = perturbations.shape
    tiles = -(-(count + 2) // SLOTS)
    domains = lax.axis_size("domain")
    up = [(i, (i + 1) % domains) for i in range(domains)]
    down = [(j, i) for i, j in up]
    level = shape_of(levels, size)
    members_f32 = shape_of(count, levels, size)
    edge_tiles = shape_of(tiles, levels, LANES)
    moment_rows = shape_of(8, LANES)
    edge_level = shape_of(levels, LANES)
    message = shape_of(-(-tiles * HALO // SLOT), levels, LANES)
    column = shape_of(levels, levels, LANES)
    work, edge_work = count * levels * size * 50, tiles * levels * LANES * 50
    scratch = [pltpu.VMEM((count, levels, size), F32)] * 2
    edge_scratch = [pltpu.VMEM((tiles, levels, LANES), F32)] * 2

    counts = obs_counts.reshape(1, size)
    low, high, low_message, high_message = call(
        pack_kernel, "pack_edges", [edge_tiles, edge_tiles, message, message],
        (perturbations, innovations, precision_field, counts),
        [
            pltpu.VMEM((count, levels, size), perturbations.dtype), pltpu.VMEM((levels, size), F32),
            pltpu.VMEM((levels, size), F32), pltpu.VMEM((1, size), jnp.int32), pltpu.SemaphoreType.DMA((4,)),
        ],
        dict.fromkeys(range(4), elsewhere), tiles * levels * LANES * 20, None,
    )
    before = lax.ppermute(low_message, "domain", up)
    after = lax.ppermute(high_message, "domain", down)
    group = max(g for g in range(1, 6) if count % g == 0)
    blocks = shape_of(group * levels, 3 * group * levels, dtype=jnp.bfloat16)
    split = pltpu.VMEM((count // group, 3 * group * levels, size), jnp.bfloat16)
    taps, square, mapped, blocks, shifted, source, weight, main = call(
        main_kernel, "first_inner",
        [
            shape_of(3, levels, LANES), column, column, blocks, shape_of(len(SHIFTS), count, levels, size, dtype=perturbations.dtype),
            level, level, level,
        ],
        (diffusivity.reshape(1, levels), vertical_map, perturbations, innovations, precision_field, counts),
        [split, scratch[0]], flops=work,
    )
    edge_members, edge_source, edge_weight, part = call(
        functools.partial(edge_kernel, count), "first_edges",
        [edge_tiles, edge_level, edge_level, shape_of(levels, size + LANES)],
        (low, high, before, after, taps, square, main), edge_scratch, flops=edge_work,
    )

    def adjoint(name, field, edge_field):
        (out,) = call(
            adjoint_kernel, name, [members_f32], (shifted, edge_members, field, edge_field, taps, mapped),
            [scratch[0], edge_scratch[0]], flops=work,
        )
        return out

    others = from_partners(part, "member")
    start = adjoint("start_vector", source, edge_source)
    first, weighted, edge_weighted, part = call(
        second_kernel, "second_apply", [level, level, edge_level, level],
        (shifted, edge_members, weight, edge_weight, taps, square, blocks, part, *others, start),
        [split, scratch[0], *edge_scratch], {11: elsewhere}, work + edge_work,
    )
    others = from_partners(part, "member")
    image = adjoint("image_vector", weighted, edge_weighted)
    second, moments = call(
        moments_kernel, "moments", [level, moment_rows],
        (source, weight, first, weighted, part, *others, image), (), {8: elsewhere},
    )
    moments = domain_terms(moments, "domain")
    return tuple(
        call(final_kernel, "combine", [members_f32, level], (*moments, start, image, first, second))
    )


def solution(mesh):
    in_specs = (
        P("member", None, "domain"),
        P(None, "domain"),
        P(None, "domain"),
        P("domain"),
        P(),
        P(),
    )
    out_specs = (P("member", None, "domain"), P(None, "domain"))
    return jax.shard_map(local, mesh=mesh, in_specs=in_specs, out_specs=out_specs, check_vma=False)
```
